128 devices in a mesh: row: 16 (over x, y), col: 8 (over z, core).
Axes of the slice: x: 4, y: 4, z: 4, core: 2. Of those that a mesh axis runs over, the one named last changes fastest.
Arguments:
- features: bfloat16 [65536, 256], P(('row', 'col')), may hold values from -6 to 6
- weight: bfloat16 [256, 256], replicated, may hold values from -0.375 to 0.375
- bias: float32 [256], replicated, may hold values from -3 to 3
- adj_blocks: bfloat16 [16, 8, 384, 128, 128], P('row', 'col'), may hold values from -0.21875 to 0.21875
- block_rows: int32 [16, 8, 384], P('row', 'col'), may hold values from 0 to 31
- block_cols: int32 [16, 8, 384], P('row', 'col'), may hold values from 0 to 63
- block_counts: int32 [16, 8], P('row', 'col'), may hold values from 96 to 384, as said below
- grad_out: bfloat16 [65536, 256], P(('row', 'col')), may hold values from -6 to 6
Outputs:
- hidden: bfloat16 [65536, 256], P(('row', 'col'))
- grad_features: bfloat16 [65536, 256], P(('row', 'col'))
- grad_weight: float32 [256, 256], replicated
- grad_bias: float32 [256], replicated
The draws below stay inside these ranges and needn't reach their ends.
Inputs may be any that keep to these rules, and one draw needn't show every extreme that they name: `block_counts`: number of used entries of each tile's block lists; exactly 384 on some tile of every draw. Entries past it are not part of A. `block_rows`: positions may repeat within a tile. `block_cols`: positions may repeat within a tile.
All inputs are finite; a program needn't handle non-finite values.
Results may differ from the reference program's by a relative error of at most 0.0075.
Values may be sent and summed in bfloat16 or wider, within the bound.
A program may use at most 192 MiB of HBM per device.

```python
import jax
import jax.numpy as jnp
from jax import lax

HID = 256
BLOCK = 128
SLAB = 512
MAXB = 384
NODES = 65536
N_ROW = 16
N_COL = 8


def draw_block_counts(key, part):
    key = jax.random.fold_in(key, 11)
    first, second = jax.random.split(key)
    divisor = jax.random.randint(first, (N_ROW, N_COL), 1, 5)
    counts = jnp.maximum(MAXB // divisor, 1).reshape(-1)
    heavy = jax.random.randint(second, (), 0, N_ROW * N_COL)
    counts = counts.at[heavy].set(MAXB)
    return counts.reshape(N_ROW, N_COL).astype(jnp.int32)


def place_ends(array, key, least, largest):
    dims = array.shape
    spot = [jax.random.randint(jax.random.fold_in(key, axis), (), 0, dims[axis]) for axis in range(len(dims))]
    array = array.at[tuple(spot)].set(least)
    longest = dims.index(max(dims))
    spot[longest] = (spot[longest] + 1) % dims[longest]
    return array.at[tuple(spot)].set(largest)


def block_levels(stream_key, extent, cuts, smallest, high):
    def one(dim, shards_of):
        draws = jax.random.uniform(jax.random.fold_in(jax.random.fold_in(stream_key, 6), dim), (shards_of,), jnp.float32, smallest / len(cuts), high / len(cuts))
        return jnp.repeat(jnp.exp(draws), extent[dim] // shards_of).reshape((-1,) + (1,) * (len(extent) - dim - 1))

    factor_of = one(*cuts[0])
    for cut in cuts[1:]:
        factor_of = factor_of * one(*cut)
    return factor_of


def noise(own_key, dims, deviation, bound, shards=(), kind=jnp.bfloat16):
    entries = deviation * jax.random.normal(own_key, dims, jnp.float32)
    if shards:
        entries = entries * block_levels(own_key, dims, shards, -0.22, 0.18)
    return jnp.clip(entries, -bound, bound).astype(kind)


def setup_inputs(seed: int = 0) -> dict:
    splits = jax.random.split(jax.random.key(seed), 9)
    features = noise(splits[0], (NODES, HID), 1.0, 6.0, ((0, 128),))
    weight = noise(splits[1], (HID, HID), HID ** -0.5, 0.375)
    bias = noise(splits[2], (HID,), 0.5, 3.0, (), jnp.float32)
    adj_blocks = noise(splits[3], (N_ROW, N_COL, MAXB, BLOCK, BLOCK), 768 ** -0.5, 0.21875, ((0, 16), (1, 8)))
    block_rows = place_ends(jax.random.randint(splits[4], (N_ROW, N_COL, MAXB), 0, N_COL * SLAB // BLOCK), jax.random.fold_in(splits[4], 1), 0, (N_COL * SLAB // BLOCK) - 1).astype(jnp.int32)
    block_cols = place_ends(jax.random.randint(splits[5], (N_ROW, N_COL, MAXB), 0, N_ROW * SLAB // BLOCK), jax.random.fold_in(splits[5], 1), 0, (N_ROW * SLAB // BLOCK) - 1).astype(jnp.int32)
    block_counts = draw_block_counts(jax.random.fold_in(splits[8], 71), 0)
    grad_out = noise(splits[7], (NODES, HID), 1.0, 6.0, ((0, 128),))
    return dict(features=features, weight=weight, bias=bias, adj_blocks=adj_blocks, block_rows=block_rows, block_cols=block_cols, block_counts=block_counts, grad_out=grad_out)


def silu_grad(value):
    sig = jax.nn.sigmoid(value)
    return sig * (1.0 + value * (1.0 - sig))

def tile_product(blocks, outer, inner, count, operand, out_blocks, transposed):
    tiles = operand.reshape(-1, BLOCK, HID)
    taken = jnp.take(tiles, inner, axis=0).astype(jnp.float32)
    values = blocks.astype(jnp.float32)
    form = 'bmk,bmf->bkf' if transposed else 'bkm,bmf->bkf'
    prod = jnp.einsum(form, values, taken, precision=lax.Precision.HIGHEST)
    live = (jnp.arange(MAXB, dtype=jnp.int32) < count).astype(jnp.float32)
    prod = prod * live[:, None, None]
    summed = jax.ops.segment_sum(prod, outer, num_segments=out_blocks)
    return summed.reshape(out_blocks * BLOCK, HID)

def reference(features, weight, bias, adj_blocks, block_rows, block_cols, block_counts, grad_out):
    rows_blk = N_COL * SLAB // BLOCK
    cols_blk = N_ROW * SLAB // BLOCK
    panel = jnp.dot(features, weight, preferred_element_type=jnp.float32).astype(jnp.bfloat16)
    grouped = panel.reshape(N_ROW, N_COL, SLAB, HID)

    def forward_row(i):

        def step(j, acc):
            operand = lax.dynamic_index_in_dim(grouped, j, 1, keepdims=False).reshape(N_ROW * SLAB, HID)
            return acc + tile_product(adj_blocks[i, j], block_rows[i, j], block_cols[i, j], block_counts[i, j], operand, rows_blk, False)
        return lax.fori_loop(0, N_COL, step, jnp.zeros((N_COL * SLAB, HID), jnp.float32))
    pre = lax.map(forward_row, jnp.arange(N_ROW, dtype=jnp.int32)).reshape(-1, HID)
    active = pre + bias
    hidden = jax.nn.silu(active).astype(jnp.bfloat16)
    grad_pre = (grad_out.astype(jnp.float32) * silu_grad(active)).astype(jnp.bfloat16)
    dgroup = grad_pre.reshape(N_ROW, N_COL * SLAB, HID)

    def backward_col(j):

        def step(i, acc):
            operand = lax.dynamic_index_in_dim(dgroup, i, 0, keepdims=False)
            return acc + tile_product(adj_blocks[i, j], block_cols[i, j], block_rows[i, j], block_counts[i, j], operand, cols_blk, True)
        return lax.fori_loop(0, N_ROW, step, jnp.zeros((N_ROW * SLAB, HID), jnp.float32))
    dcols = lax.map(backward_col, jnp.arange(N_COL, dtype=jnp.int32))
    grad_panel = dcols.reshape(N_COL, N_ROW, SLAB, HID).transpose(1, 0, 2, 3).reshape(-1, HID).astype(jnp.bfloat16)
    grad_features = lax.dot_general(grad_panel, weight, (((1,), (1,)), ((), ())), preferred_element_type=jnp.float32).astype(jnp.bfloat16)
    grad_weight = lax.dot_general(features, grad_panel, (((0,), (0,)), ((), ())), preferred_element_type=jnp.float32)
    grad_bias = lax.optimization_barrier(jnp.sum(grad_pre.astype(jnp.float32), axis=0))
    return (hidden, grad_features, grad_weight, grad_bias)
```

```python
import functools

import jax
import jax.numpy as jnp
from jax import lax
from jax.experimental import pallas as pl
from jax.experimental.pallas import tpu as pltpu
from jax.sharding import PartitionSpec as P

MESH = pl.DeviceIdType.MESH
VMEM = pltpu.VMEM
SMEM = pltpu.SMEM
BF16 = jnp.bfloat16
F32 = jnp.float32
I32 = jnp.int32
EDGE = 128
WIDE = 128
HALVES = 2
SLOTS = 512
MAXB = 384
ROW_BLOCKS = 32
COL_BLOCKS = 64
FWD_STEPS = (MAXB + ROW_BLOCKS) // 2
BWD_STEPS = (MAXB + COL_BLOCKS) // 2
UNROLL = 16
PART = 40


def dot(a, b):
    return jnp.dot(a, b, preferred_element_type=F32)


def dot_nt(a, b):
    return lax.dot_general(a, b, (((1,), (1,)), ((), ())), preferred_element_type=F32)


def dot_tn(a, b):
    return lax.dot_general(a, b, (((0,), (0,)), ((), ())), preferred_element_type=F32)


def one_table(outer, inner, count, table):
    ids = lax.broadcasted_iota(I32, (1, MAXB), 1)
    key = jnp.where(ids < count, outer, -1)
    lanes = lax.broadcasted_iota(I32, (EDGE, MAXB), 0)
    member = (lanes == key).astype(F32)
    member16 = member.astype(BF16)
    before = (
        lax.broadcasted_iota(I32, (MAXB, MAXB), 0) < lax.broadcasted_iota(I32, (MAXB, MAXB), 1)
    ).astype(F32).astype(BF16)
    within = jnp.sum(member * dot(member16, before), axis=0, keepdims=True)
    held = jnp.sum(member, axis=1, keepdims=True).astype(I32)
    pairs = ((held + 1) >> 1).astype(F32)
    start = jnp.sum((lanes < key).astype(F32) * pairs, axis=0, keepdims=True)
    place = jnp.where(key >= 0, (2.0 * start + within).astype(I32), -1)
    taken = (lax.broadcasted_iota(I32, (SLOTS, MAXB), 0) == place).astype(F32).astype(BF16)
    which = lax.broadcasted_iota(I32, (8, MAXB), 0)
    low = jnp.broadcast_to(ids & 127, (8, MAXB))
    high = jnp.broadcast_to(ids >> 7, (8, MAXB))
    operand = jnp.broadcast_to(inner, (8, MAXB))
    first = jnp.broadcast_to((within < 0.5).astype(I32), (8, MAXB))
    values = jnp.where(which == 0, low, jnp.where(which == 1, high, jnp.where(which == 2, operand, jnp.where(which == 3, first, 1))))
    picked = dot_nt(values.astype(F32).astype(BF16), taken).astype(I32)
    table[0:1, :] = jnp.where(picked[4:5, :] > 0, picked[0:1, :] + EDGE * picked[1:2, :], MAXB)
    table[1:2, :] = picked[2:3, :]
    table[2:3, :] = 1 - picked[3:4, :]
    held_row = dot_nt(jnp.ones((8, MAXB), BF16), member16).astype(I32)
    pairs_row = ((held_row + 1) >> 1).astype(F32).astype(BF16)
    upto = (
        lax.broadcasted_iota(I32, (EDGE, EDGE), 0) <= lax.broadcasted_iota(I32, (EDGE, EDGE), 1)
    ).astype(F32).astype(BF16)
    ends = jnp.maximum(dot(pairs_row, upto).astype(I32) - 1, 0)
    table[3:4, 0:EDGE] = ends[0:1, :]
    table[4:5, 0:EDGE] = (held_row[0:1, :] > 0).astype(I32)


def table_kernel(count, rows, cols, fwd, bwd):
    fwd[...] = jnp.zeros_like(fwd)
    bwd[...] = jnp.zeros_like(bwd)
    one_table(rows[0], cols[0], count[0, 0], fwd)
    one_table(cols[0], rows[0], count[0, 0], bwd)


def make_tables(block_rows, block_cols, block_counts):
    shape = jax.ShapeDtypeStruct((8, SLOTS), I32)
    return pl.pallas_call(
        table_kernel,
        out_shape=(shape, shape),
        in_specs=[pl.BlockSpec(memory_space=SMEM)] + [pl.BlockSpec(memory_space=VMEM)] * 2,
        out_specs=(pl.BlockSpec(memory_space=VMEM),) * 2,
    )(block_counts, block_rows, block_cols)


def layer_kernel(
    fwd, bwd, feat, weight, bias, blocks_hbm, gout,
    hidden, gfeat, gweight, gbias,
    blocks, x0, x1, segs, sib_out, sib_in, z_out, z_in, ax, gp, gt0, gt1,
    a_out, a_in, b_out, b_in, a2_out, a2_in, b2_out, b2_in,
    ar_mine, ar_cols, ar_x, ar_y, ar_all,
    blocks_sem, x_send, x_recv, sib_send, sib_recv, z_send, z_recv, g_send, g_recv,
    c_send, c_recv, r_send, r_recv, ar_send, ar_recv,
):
    row = lax.axis_index("row")
    col = lax.axis_index("col")
    x, y = row // 4, row % 4
    z, core = col // 2, col % 2
    xs = (x0, x1)
    gts = (gt0, gt1)

    def at_x(d):
        return (lax.rem(x + d + 4, 4) * 4 + y, col)

    def at_y(d):
        return (x * 4 + lax.rem(y + d + 4, 4), col)

    def at_z(d):
        return (row, lax.rem(z + d + 4, 4) * 2 + core)

    sibling = (row, z * 2 + 1 - core)

    def remote(src, dst, send, recv, to):
        return pltpu.make_async_remote_copy(
            src_ref=src, dst_ref=dst, send_sem=send, recv_sem=recv, device_id=to, device_id_type=MESH
        )

    load = pltpu.make_async_copy(blocks_hbm.at[0, 0], blocks.at[pl.ds(0, MAXB)], blocks_sem)
    load.start()
    barrier = pltpu.get_barrier_semaphore()
    for d in range(1, 4):
        for to in (at_x(d), at_y(d)):
            pl.semaphore_signal(barrier, inc=1, device_id=to, device_id_type=MESH)
    for d in range(1, 8):
        to = (row, lax.rem(col + d, 8))
        pl.semaphore_signal(barrier, inc=1, device_id=to, device_id_type=MESH)

    for h in range(HALVES):
        xs[h][x, y] = feat[:, h * WIDE:(h + 1) * WIDE].reshape(4, EDGE, WIDE)
    blocks[MAXB] = jnp.zeros((EDGE, EDGE), BF16)
    pl.semaphore_wait(barrier, 13)

    def slab(h, half, e, d):
        first = lax.rem((x if half == 0 else y) - e + 4, 4)
        second = lax.rem((y if half == 0 else x) - d + 4, 4)
        return (first, second) if half == 0 else (second, first)

    def x_copy(h, half, e, d, q, n, sem, to):
        i, j = slab(h, half, e, d)
        part = xs[h].at[i, j, pl.ds(q, n)]
        return remote(part, part, x_send.at[h, half, sem], x_recv.at[h, half, sem], to)

    firsts = (at_x, at_y)
    seconds = (at_y, at_x)

    def x_along(h, half, d):
        return x_copy(h, half, 0, 0, 2 * half, 2, d - 1, firsts[half](d))

    def x_across(h, half, e, way):
        return x_copy(h, half, e, 0, 2 * half, 2, 3 + e * 4 + way, seconds[half](1 - 2 * way))

    def x_pass(h, half, e, way):
        return x_copy(
            h, half, e, 1 - 2 * way, 2 * half + way, 1, 5 + e * 4 + way, seconds[half](1 - 2 * way)
        )

    def x_start(h):
        for half in range(2):
            for d in (1, 3, 2):
                x_along(h, half, d).start()
            for way in range(2):
                x_across(h, half, 0, way).start()

    def x_step(h, e):
        for half in range(2):
            x_along(h, half, e).wait_recv()
            for way in range(2):
                x_across(h, half, e, way).start()

    def x_forward(h, e):
        for half in range(2):
            for way in range(2):
                x_across(h, half, e, way).wait_recv()
                x_pass(h, half, e, way).start()

    def x_finish(h):
        for e in range(4):
            for half in range(2):
                for way in range(2):
                    x_pass(h, half, e, way).wait_recv()

    def x_drain(h):
        for half in range(2):
            for d in (1, 2, 3):
                x_along(h, half, d).wait_send()
            for e in range(4):
                for way in range(2):
                    x_across(h, half, e, way).wait_send()
                    x_pass(h, half, e, way).wait_send()

    def products(table, steps, one, between):
        trips = steps // UNROLL
        cuts = [trips * i // len(between) for i in range(len(between) + 1)]

        def trip(i, acc):
            for u in range(UNROLL):
                k = i * UNROLL + u
                keep = table[2, 2 * k].astype(F32)
                acc = acc * keep + one(table[0, 2 * k], table[0, 2 * k + 1], table[1, 2 * k], table[1, 2 * k + 1])
                segs[k] = acc.astype(BF16)
            return acc

        acc = jnp.zeros((EDGE, WIDE), F32)
        for i, act in enumerate(between):
            act()
            acc = lax.fori_loop(cuts[i], cuts[i + 1], trip, acc)

    def forward(h, between):
        def one(b0, b1, c0, c1):
            i0, j0, q0 = c0 // 16, (c0 // 4) % 4, c0 % 4
            i1, j1, q1 = c1 // 16, (c1 // 4) % 4, c1 % 4
            pair = jnp.concatenate([blocks[b0], blocks[b1]], axis=1)
            taken = jnp.concatenate([xs[h][i0, j0, q0], xs[h][i1, j1, q1]], axis=0)
            return dot(pair, taken)

        products(fwd, FWD_STEPS, one, between)

    def backward(h, between):
        def one(b0, b1, r0, r1):
            pair = jnp.concatenate([blocks[b0], blocks[b1]], axis=0)
            taken = jnp.concatenate(
                [gts[h][r0 // 4, r0 % 4], gts[h][r1 // 4, r1 % 4]], axis=1
            )
            return dot(taken, pair)

        products(bwd, BWD_STEPS, one, between)

    def segment(table, r):
        return segs[table[3, r]] * table[4, r].astype(F32).astype(BF16)

    def sib_copy(h, d):
        return remote(sib_out.at[h, d], sib_in.at[h, d], sib_send.at[h, d], sib_recv.at[h, d], sibling)

    def z_copy(h, d):
        return remote(z_out.at[h, d], z_in.at[h, d], z_send.at[h, d], z_recv.at[h, d], at_z(d))

    def sum_start(h):
        for d in (1, 3, 2, 0):
            zz = lax.rem(z + d, 4)
            for q in range(4):
                sib_out[h, d, q] = segment(fwd, (zz * 2 + 1 - core) * 4 + q)
            sib_copy(h, d).start()
        for d in (1, 3, 2, 0):
            zz = lax.rem(z + d, 4)
            for q in range(4):
                z_out[h, d, q] = segment(fwd, (zz * 2 + core) * 4 + q)

    def sum_step(h):
        for d in (1, 3, 2):
            sib_copy(h, d).wait_recv()
            for q in range(4):
                z_out[h, d, q] = (z_out[h, d, q].astype(F32) + sib_in[h, d, q].astype(F32)).astype(BF16)
            z_copy(h, d).start()
        sib_copy(h, 0).wait_recv()

    def sum_finish(h):
        for d in (1, 3, 2):
            z_copy(h, d).wait_recv()
        for q in range(4):
            total = z_out[h, 0, q].astype(F32) + sib_in[h, 0, q].astype(F32)
            for d in (1, 3, 2):
                total = total + z_in[h, d, q].astype(F32)
            ax[q * EDGE:(q + 1) * EDGE, h * WIDE:(h + 1) * WIDE] = total

    def g_part(h, d, k):
        return gts[h].at[lax.rem(z + d + 4, 4) * 2 + k]

    def g_across(h, d):
        part = g_part(h, 0, core)
        return remote(part, part, g_send.at[h, d - 1], g_recv.at[h, d - 1], at_z(d))

    def g_sibling(h, d):
        part = g_part(h, -d, core)
        return remote(part, part, g_send.at[h, 3 + d], g_recv.at[h, 3 + d], sibling)

    def g_start(h):
        for d in (1, 3, 2):
            g_across(h, d).start()
        g_sibling(h, 0).start()

    def g_step(h):
        for d in (1, 3, 2):
            g_across(h, d).wait_recv()
            g_sibling(h, d).start()
        for d in (0, 1, 3, 2):
            g_sibling(h, d).wait_recv()

    outs, ins = (a_out, b_out), (a_in, b_in)
    outs2, ins2 = (a2_out, b2_out), (a2_in, b2_in)

    def c_copy(h, half, d):
        return remote(
            outs[half].at[h, d], ins[half].at[h, d], c_send.at[h, half, d], c_recv.at[h, half, d], firsts[half](d)
        )

    def r_copy(h, half, d):
        return remote(
            outs2[half].at[h, d], ins2[half].at[h, d], r_send.at[h, half, d], r_recv.at[h, half, d], seconds[half](d)
        )

    def back_gather(h, d):
        for half in range(2):
            for s in range(4):
                first = lax.rem((x if half == 0 else y) + d, 4)
                second = lax.rem((y if half == 0 else x) + s, 4)
                i, j = (first, second) if half == 0 else (second, first)
                for q in range(2):
                    outs[half][h, d, s, q] = segment(bwd, (i * 4 + j) * 4 + 2 * half + q)

    def back_start(h):
        for d in (1, 3, 2):
            back_gather(h, d)
            for half in range(2):
                c_copy(h, half, d).start()
        back_gather(h, 0)

    def back_step(h):
        for half in range(2):
            for d in (1, 3, 2):
                c_copy(h, half, d).wait_recv()
        for s in (1, 3, 2, 0):
            for half in range(2):
                for q in range(2):
                    total = outs[half][h, 0, s, q].astype(F32)
                    for d in (1, 3, 2):
                        total = total + ins[half][h, d, s, q].astype(F32)
                    outs2[half][h, s, q] = total.astype(BF16)
                if s:
                    r_copy(h, half, s).start()

    def back_finish(h):
        for half in range(2):
            for d in (1, 3, 2):
                r_copy(h, half, d).wait_recv()
            for q in range(2):
                total = outs2[half][h, 0, q].astype(F32)
                for d in (1, 3, 2):
                    total = total + ins2[half][h, d, q].astype(F32)
                b = 2 * half + q
                gfeat[b * EDGE:(b + 1) * EDGE, h * WIDE:(h + 1) * WIDE] = jnp.transpose(total).astype(BF16)

    def ar_scatter(d):
        to = lax.rem(col + d, 8)
        return remote(ar_mine.at[to], ar_cols.at[col], ar_send.at[d], ar_recv.at[d], (row, to))

    def ar_over_x(d):
        return remote(ar_x.at[x], ar_x.at[x], ar_send.at[7 + d], ar_recv.at[7 + d], at_x(d))

    def ar_over_y(d):
        return remote(ar_y.at[y], ar_y.at[y], ar_send.at[10 + d], ar_recv.at[10 + d], at_y(d))

    def ar_gather(d):
        to = lax.rem(col + d, 8)
        return remote(ar_all.at[col], ar_all.at[col], ar_send.at[13 + d], ar_recv.at[13 + d], (row, to))

    def ar_start():
        for d in range(1, 8):
            ar_scatter(d).start()
        ar_cols[col] = ar_mine[col]

    def ar_step1():
        for d in range(1, 8):
            ar_scatter(d).wait_recv()
        total = ar_cols[0]
        for i in range(1, 8):
            total = total + ar_cols[i]
        ar_x[x] = total
        for d in range(1, 4):
            ar_over_x(d).start()

    def ar_step2():
        for d in range(1, 4):
            ar_over_x(d).wait_recv()
        ar_y[y] = (ar_x[0] + ar_x[1]) + (ar_x[2] + ar_x[3])
        for d in range(1, 4):
            ar_over_y(d).start()

    def ar_step3():
        for d in range(1, 4):
            ar_over_y(d).wait_recv()
        ar_all[col] = (ar_y[0] + ar_y[1]) + (ar_y[2] + ar_y[3])
        for d in range(1, 8):
            ar_gather(d).start()

    def ar_finish():
        for d in range(1, 8):
            ar_gather(d).wait_recv()
        for i in range(8):
            gweight[i * 32:(i + 1) * 32, :] = ar_all[i, 0:32, :]
        gbias[...] = ar_all[0, 32:33, :]

    def nothing():
        pass

    x_start(0)
    for e in (1, 3, 2):
        x_step(0, e)
    x_start(1)
    for e in (0, 1, 3, 2):
        x_forward(0, e)
    for e in (1, 3, 2):
        x_step(1, e)
    x_finish(0)
    load.wait()
    forward(0, [functools.partial(x_forward, 1, e) for e in (0, 1, 3, 2)] + [nothing])
    sum_start(0)
    sum_step(0)
    x_finish(1)
    forward(1, [nothing])
    sum_start(1)
    sum_finish(0)
    sum_step(1)
    sum_finish(1)

    bias_sum = jnp.zeros((1, HALVES * WIDE), F32)
    for q in range(4):
        at = slice(q * EDGE, (q + 1) * EDGE)
        total = ax[at, :]
        high = total.astype(BF16)
        low = (total - high.astype(F32)).astype(BF16)
        value = dot(high, weight[...]) + dot(low, weight[...]) + bias[...]
        sig = 1.0 / (1.0 + jnp.exp(-value))
        grad = (gout[at, :].astype(F32) * (sig * (1.0 + value * (1.0 - sig)))).astype(BF16)
        hidden[at, :] = (value * sig).astype(BF16)
        gp[at, :] = grad
        bias_sum = bias_sum + jnp.sum(grad.astype(F32), axis=0, keepdims=True)
        turned = dot_nt(weight[...], grad).astype(BF16)
        for h in range(HALVES):
            gts[h][col, q] = turned[h * WIDE:(h + 1) * WIDE, :]
    g_start(0)
    g_start(1)
    total = ax[...]
    high = total.astype(BF16)
    low = (total - high.astype(F32)).astype(BF16)
    weight_term = dot_tn(high, gp[...]) + dot_tn(low, gp[...])
    for i in range(8):
        ar_mine[i, 0:32, :] = weight_term[i * 32:(i + 1) * 32, :]
        ar_mine[i, 32:PART, :] = jnp.broadcast_to(bias_sum, (PART - 32, HALVES * WIDE))
    g_step(0)
    ar_start()
    backward(0, [nothing])
    back_start(0)
    ar_step1()
    g_step(1)
    backward(1, [nothing, ar_step2, ar_step3])
    back_start(1)
    back_step(0)
    ar_finish()
    back_finish(0)
    back_step(1)
    back_finish(1)

    for h in range(HALVES):
        x_drain(h)
        for d in range(4):
            sib_copy(h, d).wait_send()
            g_sibling(h, d).wait_send()
        for d in range(1, 4):
            z_copy(h, d).wait_send()
            g_across(h, d).wait_send()
            for half in range(2):
                c_copy(h, half, d).wait_send()
                r_copy(h, half, d).wait_send()
    for d in range(1, 4):
        ar_over_x(d).wait_send()
        ar_over_y(d).wait_send()
    for d in range(1, 8):
        ar_scatter(d).wait_send()
        ar_gather(d).wait_send()


def body(features, weight, bias, adj_blocks, block_rows, block_cols, block_counts, grad_out):
    nodes, hid = features.shape
    fwd, bwd = make_tables(block_rows, block_cols, block_counts)
    sem = pltpu.SemaphoreType.DMA
    block = (EDGE, EDGE)
    vmem = pl.BlockSpec(memory_space=VMEM)
    smem = pl.BlockSpec(memory_space=SMEM)
    hidden, grad_features, grad_weight, grad_bias = pl.pallas_call(
        layer_kernel,
        out_shape=(
            jax.ShapeDtypeStruct((nodes, hid), BF16),
            jax.ShapeDtypeStruct((nodes, hid), BF16),
            jax.ShapeDtypeStruct((hid, hid), F32),
            jax.ShapeDtypeStruct((1, hid), F32),
        ),
        in_specs=[smem, smem, vmem, vmem, vmem, pl.BlockSpec(memory_space=pl.ANY), vmem],
        out_specs=(vmem,) * 4,
        scratch_shapes=[
            VMEM((MAXB + 8, EDGE, EDGE), BF16),
            VMEM((4, 4, 4) + block, BF16),
            VMEM((4, 4, 4) + block, BF16),
            VMEM((BWD_STEPS,) + block, BF16),
            VMEM((HALVES, 4, 4) + block, BF16),
            VMEM((HALVES, 4, 4) + block, BF16),
            VMEM((HALVES, 4, 4) + block, BF16),
            VMEM((HALVES, 4, 4) + block, BF16),
            VMEM((nodes, hid), F32),
            VMEM((nodes, hid), BF16),
            VMEM((8, 4) + block, BF16),
            VMEM((8, 4) + block, BF16),
            VMEM((HALVES, 4, 4, 2) + block, BF16),
            VMEM((HALVES, 4, 4, 2) + block, BF16),
            VMEM((HALVES, 4, 4, 2) + block, BF16),
            VMEM((HALVES, 4, 4, 2) + block, BF16),
            VMEM((HALVES, 4, 2) + block, BF16),
            VMEM((HALVES, 4, 2) + block, BF16),
            VMEM((HALVES, 4, 2) + block, BF16),
            VMEM((HALVES, 4, 2) + block, BF16),
            VMEM((8, PART, hid), F32),
            VMEM((8, PART, hid), F32),
            VMEM((4, PART, hid), F32),
            VMEM((4, PART, hid), F32),
            VMEM((8, PART, hid), F32),
            sem,
            sem((HALVES, 2, 19)), sem((HALVES, 2, 19)),
            sem((HALVES, 4)), sem((HALVES, 4)),
            sem((HALVES, 4)), sem((HALVES, 4)),
            sem((HALVES, 7)), sem((HALVES, 7)),
            sem((HALVES, 2, 4)), sem((HALVES, 2, 4)),
            sem((HALVES, 2, 4)), sem((HALVES, 2, 4)),
            sem((21,)), sem((21,)),
        ],
        compiler_params=pltpu.CompilerParams(
            collective_id=0, has_side_effects=True, vmem_limit_bytes=56 * 2**20
        ),
        cost_estimate=pl.CostEstimate(flops=8 * 10**9, bytes_accessed=16 * 2**20, transcendentals=2**18),
    )(fwd, bwd, features, weight, bias.reshape(1, hid), adj_blocks, grad_out)
    return hidden, grad_features, grad_weight, grad_bias.reshape(hid)


def solution(mesh):
    in_specs = (
        P(("row", "col"), None),
        P(),
        P(),
        P("row", "col", None, None, None),
        P("row", "col", None),
        P("row", "col", None),
        P("row", "col"),
        P(("row", "col"), None),
    )
    out_specs = (P(("row", "col"), None), P(("row", "col"), None), P(), P())
    return jax.shard_map(body, mesh=mesh, in_specs=in_specs, out_specs=out_specs, check_vma=False)
```

```python
import functools

import jax
import jax.numpy as jnp
from jax import lax
from jax.experimental import pallas as pl
from jax.experimental.pallas import tpu as pltpu
from jax.sharding import PartitionSpec as P

MESH = pl.DeviceIdType.MESH
VMEM = pltpu.VMEM
SMEM = pltpu.SMEM
BF16 = jnp.bfloat16
F32 = jnp.float32
I32 = jnp.int32
EDGE = 128
WIDE = 128
HALVES = 2
THIN = 64
CHUNKS = 4
SLOTS = 512
MAXB = 384
ROW_BLOCKS = 32
COL_BLOCKS = 64
FWD_STEPS = (MAXB + ROW_BLOCKS) // 2
BWD_STEPS = (MAXB + COL_BLOCKS) // 2
FWD_UNROLL = 26
BWD_UNROLL = 32
PART = 40


def dot(a, b):
    return jnp.dot(a, b, preferred_element_type=F32)


def dot_nt(a, b):
    return lax.dot_general(a, b, (((1,), (1,)), ((), ())), preferred_element_type=F32)


def dot_tn(a, b):
    return lax.dot_general(a, b, (((0,), (0,)), ((), ())), preferred_element_type=F32)


def one_table(outer, inner, count, table):
    ids = lax.broadcasted_iota(I32, (1, MAXB), 1)
    key = jnp.where(ids < count, outer, -1)
    turn = jnp.transpose(jnp.broadcast_to(key, (8, MAXB)))[:, 0:1]
    ones = jnp.ones((MAXB, MAXB), I32)
    earlier = lax.broadcasted_iota(I32, (MAXB, MAXB), 0) < lax.broadcasted_iota(I32, (MAXB, MAXB), 1)
    within = jnp.sum(jnp.where((turn == key) & earlier, ones, 0), axis=0, keepdims=True)
    lanes = lax.broadcasted_iota(I32, (MAXB, EDGE), 1)
    held = jnp.sum(jnp.where(turn == lanes, 1, 0), axis=0, keepdims=True)
    pairs = (held + 1) >> 1
    pairs_turn = jnp.transpose(jnp.broadcast_to(pairs, (8, EDGE)))[:, 0:1]
    rows = lax.broadcasted_iota(I32, (EDGE, EDGE), 0)
    upto = jnp.sum(jnp.where(rows <= lax.broadcasted_iota(I32, (EDGE, EDGE), 1), pairs_turn, 0), axis=0, keepdims=True)
    under = lax.broadcasted_iota(I32, (EDGE, MAXB), 0) < key
    start = jnp.sum(jnp.where(under, pairs_turn, 0), axis=0, keepdims=True)
    place = jnp.where(key >= 0, 2 * start + within, -1)
    packed = (ids + 1) + 512 * inner + jnp.where(within == 0, 65536, 0)
    place_turn = jnp.transpose(jnp.broadcast_to(place, (8, MAXB)))[:, 0:1]
    packed_turn = jnp.transpose(jnp.broadcast_to(packed, (8, MAXB)))[:, 0:1]
    taken = place_turn == lax.broadcasted_iota(I32, (MAXB, SLOTS), 1)
    picked = jnp.sum(jnp.where(taken, packed_turn, 0), axis=0, keepdims=True)
    block = picked & 511
    table[0:1, :] = jnp.where(block > 0, block - 1, MAXB)
    table[1:2, :] = (picked >> 9) & 63
    table[2:3, :] = 1 - (picked >> 16)
    table[3:4, :] = jnp.broadcast_to(jnp.concatenate([jnp.maximum(upto - 1, 0)] * 4, axis=1), (1, SLOTS))
    table[4:5, :] = jnp.concatenate([jnp.minimum(held, 1)] * 4, axis=1)
    table[5:8, :] = jnp.zeros((3, SLOTS), I32)


def layer_kernel(
    count, rows, cols, feat_hbm, weight_hbm, bias, blocks_hbm, gout_hbm,
    hidden_hbm, gfeat_hbm, gweight_hbm, gbias_hbm,
    weight, gout, hidden, gfeat, gweight, gbias,
    fwd, bwd, fwd_made, bwd_made,
    blocks, x0, x1, segs, segs2, sib_out, sib_in, z_out, z_in, ax, gp, gt0, gt1, gt2, gt3,
    f_out, f_in, c_out, c_in, own, r_out, r_in,
    ar_mine, ar_cols, ar_x, ar_y, ar_all,
    blocks_sem, feat_sem, table_sem, other_sem, out_sem, x_send, x_recv, sib_send, sib_recv, z_send, z_recv, g_send, g_recv,
    c_send, c_recv, r_send, r_recv, ar_send, ar_recv,
):
    row = lax.axis_index("row")
    col = lax.axis_index("col")
    x, y = row // 4, row % 4
    z, core = col // 2, col % 2
    xs = (x0, x1)
    gts = (gt0, gt1, gt2, gt3)

    def at_x(d):
        return (lax.rem(x + d + 4, 4) * 4 + y, col)

    def at_y(d):
        return (x * 4 + lax.rem(y + d + 4, 4), col)

    def at_z(d):
        return (row, lax.rem(z + d + 4, 4) * 2 + core)

    sibling = (row, z * 2 + 1 - core)

    def remote(src, dst, send, recv, to):
        return pltpu.make_async_remote_copy(
            src_ref=src, dst_ref=dst, send_sem=send, recv_sem=recv, device_id=to, device_id_type=MESH
        )

    load = pltpu.make_async_copy(blocks_hbm.at[0, 0], blocks.at[pl.ds(0, MAXB)], blocks_sem)
    base = (x * 4 + y) * 4
    feats = [
        pltpu.make_async_copy(
            feat_hbm.at[:, :, pl.ds(h * WIDE, WIDE)], xs[h].at[pl.ds(base, 4)], feat_sem.at[h]
        )
        for h in range(HALVES)
    ]
    for copy in feats:
        copy.start()
    others = [
        pltpu.make_async_copy(weight_hbm, weight, other_sem.at[0]),
        pltpu.make_async_copy(gout_hbm, gout, other_sem.at[1]),
    ]
    for copy in others:
        copy.start()
    load.start()
    results = [
        pltpu.make_async_copy(ref, hbm, out_sem.at[i])
        for i, (ref, hbm) in enumerate(
            ((hidden, hidden_hbm), (gfeat, gfeat_hbm), (gweight, gweight_hbm), (gbias, gbias_hbm))
        )
    ]
    barrier = pltpu.get_barrier_semaphore()
    for d in range(1, 4):
        for to in (at_x(d), at_y(d)):
            pl.semaphore_signal(barrier, inc=1, device_id=to, device_id_type=MESH)
    for d in range(1, 8):
        to = (row, lax.rem(col + d, 8))
        pl.semaphore_signal(barrier, inc=1, device_id=to, device_id_type=MESH)

    pl.semaphore_wait(barrier, 13)

    def slab(h, half, e, d):
        first = lax.rem((x if half == 0 else y) - e + 4, 4)
        second = lax.rem((y if half == 0 else x) - d + 4, 4)
        return (first, second) if half == 0 else (second, first)

    def x_copy(h, half, e, d, q, n, sem, to):
        i, j = slab(h, half, e, d)
        part = xs[h].at[pl.ds((i * 4 + j) * 4 + q, n)]
        return remote(part, part, x_send.at[h, half, sem], x_recv.at[h, half, sem], to)

    firsts = (at_x, at_y)
    seconds = (at_y, at_x)

    def x_along(h, half, d):
        return x_copy(h, half, 0, 0, 2 * half, 2, d - 1, firsts[half](d))

    def x_across(h, half, e, way):
        return x_copy(h, half, e, 0, 2 * half, 2, 3 + e * 4 + way, seconds[half](1 - 2 * way))

    def x_pass(h, half, e, way):
        return x_copy(
            h, half, e, 1 - 2 * way, 2 * half + way, 1, 5 + e * 4 + way, seconds[half](1 - 2 * way)
        )

    def x_start(h):
        for half in range(2):
            for d in (1, 3, 2):
                x_along(h, half, d).start()
            for way in range(2):
                x_across(h, half, 0, way).start()

    def x_step(h, e):
        for half in range(2):
            x_along(h, half, e).wait_recv()
            for way in range(2):
                x_across(h, half, e, way).start()

    def x_forward(h, e):
        for half in range(2):
            for way in range(2):
                x_across(h, half, e, way).wait_recv()
                x_pass(h, half, e, way).start()

    def x_finish(h):
        for e in range(4):
            for half in range(2):
                for way in range(2):
                    x_pass(h, half, e, way).wait_recv()

    def x_drain(h):
        for half in range(2):
            for d in (1, 2, 3):
                x_along(h, half, d).wait_send()
            for e in range(4):
                for way in range(2):
                    x_across(h, half, e, way).wait_send()
                    x_pass(h, half, e, way).wait_send()

    def products(table, steps, unroll, wide, one, out, between):
        trips = steps // unroll
        cuts = [trips * i // len(between) for i in range(len(between) + 1)]

        def trip(i, acc):
            for u in range(unroll):
                k = i * unroll + u
                keep = table[2, 2 * k].astype(F32)
                acc = acc * keep + one(table[0, 2 * k], table[0, 2 * k + 1], table[1, 2 * k], table[1, 2 * k + 1])
                out[k] = acc.astype(BF16)
            return acc

        acc = jnp.zeros((wide, EDGE), F32)
        for i, act in enumerate(between):
            act()
            acc = lax.fori_loop(cuts[i], cuts[i + 1], trip, acc)

    def forward(h, between):
        def one(b0, b1, c0, c1):
            pair = jnp.concatenate([blocks[b0], blocks[b1]], axis=1)
            taken = jnp.concatenate([xs[h][c0], xs[h][c1]], axis=0)
            return dot(pair, taken)

        products(fwd, FWD_STEPS, FWD_UNROLL, EDGE, one, segs, between)

    def backward(h, between):
        def one(b0, b1, r0, r1):
            pair = jnp.concatenate([blocks[b0], blocks[b1]], axis=0)
            taken = jnp.concatenate([gts[h][r0], gts[h][r1]], axis=1)
            return dot(taken, pair)

        products(bwd, BWD_STEPS, BWD_UNROLL, THIN, one, segs2, between)

    def segment(table, out, r):
        return out[table[3, r]] * table[4, r].astype(F32).astype(BF16)

    def sib_copy(h, d):
        return remote(sib_out.at[h, d], sib_in.at[h, d], sib_send.at[h, d], sib_recv.at[h, d], sibling)

    def z_copy(h, d):
        return remote(z_out.at[h, d], z_in.at[h, d], z_send.at[h, d], z_recv.at[h, d], at_z(d))

    def sum_start(h):
        for d in (1, 3, 2, 0):
            zz = lax.rem(z + d, 4)
            for q in range(4):
                sib_out[h, d, q] = segment(fwd, segs, (zz * 2 + 1 - core) * 4 + q)
            sib_copy(h, d).start()
        for d in (1, 3, 2, 0):
            zz = lax.rem(z + d, 4)
            for q in range(4):
                z_out[h, d, q] = segment(fwd, segs, (zz * 2 + core) * 4 + q)

    def sum_step(h):
        for d in (1, 3, 2):
            sib_copy(h, d).wait_recv()
            for q in range(4):
                z_out[h, d, q] = (z_out[h, d, q].astype(F32) + sib_in[h, d, q].astype(F32)).astype(BF16)
            z_copy(h, d).start()
        sib_copy(h, 0).wait_recv()

    def sum_finish(h):
        for d in (1, 3, 2):
            z_copy(h, d).wait_recv()
        for q in range(4):
            total = z_out[h, 0, q].astype(F32) + sib_in[h, 0, q].astype(F32)
            for d in (1, 3, 2):
                total = total + z_in[h, d, q].astype(F32)
            ax[q * EDGE:(q + 1) * EDGE, h * WIDE:(h + 1) * WIDE] = total

    def g_part(h, d, k):
        return gts[h].at[pl.ds((lax.rem(z + d + 4, 4) * 2 + k) * 4, 4)]

    def g_across(h, d):
        part = g_part(h, 0, core)
        return remote(part, part, g_send.at[h, d - 1], g_recv.at[h, d - 1], at_z(d))

    def g_sibling(h, d):
        part = g_part(h, -d, core)
        return remote(part, part, g_send.at[h, 3 + d], g_recv.at[h, 3 + d], sibling)

    def g_start(h):
        for d in (1, 3, 2):
            g_across(h, d).start()
        g_sibling(h, 0).start()

    def g_step(h):
        for d in (1, 3, 2):
            g_across(h, d).wait_recv()
            g_sibling(h, d).start()
        for d in (0, 1, 3, 2):
            g_sibling(h, d).wait_recv()

    def f_copy(h, half, way):
        return remote(
            f_out.at[h, half, way], f_in.at[h, half, way],
            c_send.at[h, half, way], c_recv.at[h, half, way], firsts[half](1 - 2 * way),
        )

    def c_copy(h, half, way, q):
        return remote(
            c_out.at[h, half, way, q], c_in.at[h, half, way, q],
            c_send.at[h, half, 2 + 2 * way + q], c_recv.at[h, half, 2 + 2 * way + q], firsts[half](1 - 2 * way),
        )

    def r_copy(h, half, d):
        return remote(
            r_out.at[h, half, d], r_in.at[h, half, d], r_send.at[h, half, d], r_recv.at[h, half, d], seconds[half](d)
        )

    def back_gather(half, d, q, to):
        for s in range(4):
            first = lax.rem((x if half == 0 else y) + d + 4, 4)
            second = lax.rem((y if half == 0 else x) + s, 4)
            i, j = (first, second) if half == 0 else (second, first)
            to[s] = segment(bwd, segs2, (i * 4 + j) * 4 + 2 * half + q)

    def back_start(h):
        for half in range(2):
            for way in range(2):
                back_gather(half, 2, way, f_out.at[h, half, way])
                f_copy(h, half, way).start()
        for half in range(2):
            for way in range(2):
                back_gather(half, 1 - 2 * way, 1 - way, c_out.at[h, half, way, 1 - way])
                c_copy(h, half, way, 1 - way).start()
        for half in range(2):
            for way in range(2):
                back_gather(half, 1 - 2 * way, way, c_out.at[h, half, way, way])
        for half in range(2):
            for q in range(2):
                back_gather(half, 0, q, own.at[h, half, q])

    def back_pass(h):
        for half in range(2):
            for way in range(2):
                f_copy(h, half, way).wait_recv()
                for s in range(4):
                    c_out[h, half, way, way, s] = (
                        c_out[h, half, way, way, s].astype(F32) + f_in[h, half, way, s].astype(F32)
                    ).astype(BF16)
                c_copy(h, half, way, way).start()

    def back_step(h):
        for half in range(2):
            for way in range(2):
                for q in range(2):
                    c_copy(h, half, way, q).wait_recv()
            for s in (2, 1, 3, 0):
                for q in range(2):
                    total = own[h, half, q, s].astype(F32)
                    total = total + c_in[h, half, 0, q, s].astype(F32) + c_in[h, half, 1, q, s].astype(F32)
                    r_out[h, half, s, q] = total.astype(BF16)
                if s:
                    r_copy(h, half, s).start()

    def back_finish(h):
        for half in range(2):
            for d in (1, 3, 2):
                r_copy(h, half, d).wait_recv()
            for q in range(2):
                total = r_out[h, half, 0, q].astype(F32)
                for d in (1, 3, 2):
                    total = total + r_in[h, half, d, q].astype(F32)
                b = 2 * half + q
                gfeat[b * EDGE:(b + 1) * EDGE, h * THIN:(h + 1) * THIN] = jnp.transpose(total).astype(BF16)

    def ar_scatter(d):
        to = lax.rem(col + d, 8)
        return remote(ar_mine.at[to], ar_cols.at[col], ar_send.at[d], ar_recv.at[d], (row, to))

    def ar_over_x(d):
        return remote(ar_x.at[x], ar_x.at[x], ar_send.at[7 + d], ar_recv.at[7 + d], at_x(d))

    def ar_over_y(d):
        return remote(ar_y.at[y], ar_y.at[y], ar_send.at[10 + d], ar_recv.at[10 + d], at_y(d))

    def ar_gather(d):
        to = lax.rem(col + d, 8)
        return remote(ar_all.at[col], ar_all.at[col], ar_send.at[13 + d], ar_recv.at[13 + d], (row, to))

    def ar_start():
        for d in range(1, 8):
            ar_scatter(d).start()
        ar_cols[col] = ar_mine[col]

    def ar_step1():
        for d in range(1, 8):
            ar_scatter(d).wait_recv()
        total = ar_cols[0]
        for i in range(1, 8):
            total = total + ar_cols[i]
        ar_x[x] = total
        for d in range(1, 4):
            ar_over_x(d).start()

    def ar_step2():
        for d in range(1, 4):
            ar_over_x(d).wait_recv()
        ar_y[y] = (ar_x[0] + ar_x[1]) + (ar_x[2] + ar_x[3])
        for d in range(1, 4):
            ar_over_y(d).start()

    def ar_step3():
        for d in range(1, 4):
            ar_over_y(d).wait_recv()
        ar_all[col] = (ar_y[0] + ar_y[1]) + (ar_y[2] + ar_y[3])
        for d in range(1, 8):
            ar_gather(d).start()

    def ar_finish():
        for d in range(1, 8):
            ar_gather(d).wait_recv()
        for i in range(8):
            gweight[i * 32:(i + 1) * 32, :] = ar_all[i, 0:32, :]
        gbias[...] = ar_all[0, 32:33, :]

    def nothing():
        pass

    feats[0].wait()
    x_start(0)
    feats[1].wait()
    x_start(1)
    blocks[MAXB] = jnp.zeros((EDGE, EDGE), BF16)
    one_table(rows[0], cols[0], count[0:1, 0:1], fwd_made)
    put_fwd = pltpu.make_async_copy(fwd_made, fwd, table_sem.at[0])
    put_fwd.start()
    for e in (1, 3, 2):
        x_step(0, e)
    one_table(cols[0], rows[0], count[0:1, 0:1], bwd_made)
    put_bwd = pltpu.make_async_copy(bwd_made, bwd, table_sem.at[1])
    put_bwd.start()
    for e in (0, 1, 3, 2):
        x_forward(0, e)
    for e in (1, 3, 2):
        x_step(1, e)
    x_finish(0)
    put_fwd.wait()
    put_bwd.wait()
    load.wait()
    for copy in others:
        copy.wait()
    forward(0, [functools.partial(x_forward, 1, e) for e in (0, 1, 3, 2)] + [nothing])
    sum_start(0)
    sum_step(0)
    x_finish(1)
    forward(1, [nothing])
    sum_start(1)
    sum_finish(0)
    sum_step(1)
    sum_finish(1)

    bias_sum = jnp.zeros((1, HALVES * WIDE), F32)
    for q in range(4):
        at = slice(q * EDGE, (q + 1) * EDGE)
        total = ax[at, :]
        high = total.astype(BF16)
        low = (total - high.astype(F32)).astype(BF16)
        value = dot(high, weight[...]) + dot(low, weight[...]) + bias[...]
        sig = 1.0 / (1.0 + jnp.exp(-value))
        grad = (gout[at, :].astype(F32) * (sig * (1.0 + value * (1.0 - sig)))).astype(BF16)
        hidden[at, :] = (value * sig).astype(BF16)
        gp[at, :] = grad
        bias_sum = bias_sum + jnp.sum(grad.astype(F32), axis=0, keepdims=True)
        turned = dot_nt(weight[...], grad).astype(BF16)
        for h in range(CHUNKS):
            gts[h][col * 4 + q] = turned[h * THIN:(h + 1) * THIN, :]
    for h in range(CHUNKS):
        g_start(h)
    total = ax[...]
    high = total.astype(BF16)
    low = (total - high.astype(F32)).astype(BF16)
    weight_term = dot_tn(high, gp[...]) + dot_tn(low, gp[...])
    for i in range(8):
        ar_mine[i, 0:32, :] = weight_term[i * 32:(i + 1) * 32, :]
        ar_mine[i, 32:PART, :] = jnp.broadcast_to(bias_sum, (PART - 32, HALVES * WIDE))
    results[0].start()
    g_step(0)
    backward(0, [nothing])
    back_start(0)
    ar_start()
    g_step(1)
    backward(1, [nothing])
    back_pass(0)
    back_start(1)
    ar_step1()
    g_step(2)
    backward(2, [nothing])
    back_pass(1)
    back_step(0)
    back_start(2)
    ar_step2()
    g_step(3)
    backward(3, [nothing])
    back_pass(2)
    back_step(1)
    back_start(3)
    ar_step3()
    back_finish(0)
    back_pass(3)
    back_step(2)
    back_finish(1)
    ar_finish()
    results[2].start()
    results[3].start()
    back_step(3)
    back_finish(2)
    back_finish(3)
    results[1].start()

    for h in range(HALVES):
        x_drain(h)
        for d in range(4):
            sib_copy(h, d).wait_send()
        for d in range(1, 4):
            z_copy(h, d).wait_send()
    for h in range(CHUNKS):
        for d in range(4):
            g_sibling(h, d).wait_send()
        for d in range(1, 4):
            g_across(h, d).wait_send()
            for half in range(2):
                r_copy(h, half, d).wait_send()
        for half in range(2):
            for way in range(2):
                f_copy(h, half, way).wait_send()
                for q in range(2):
                    c_copy(h, half, way, q).wait_send()
    for d in range(1, 4):
        ar_over_x(d).wait_send()
        ar_over_y(d).wait_send()
    for d in range(1, 8):
        ar_scatter(d).wait_send()
        ar_gather(d).wait_send()
    for copy in results:
        copy.wait()


def hand_on_kernel(*refs):
    n = len(refs) // 3
    given, out, held, sems = refs[:n], refs[n:2 * n], refs[2 * n:3 * n], refs[3 * n]
    reads = [pltpu.make_async_copy(given[i], held[i], sems.at[0, i]) for i in range(n)]
    writes = [pltpu.make_async_copy(held[i], out[i], sems.at[1, i]) for i in range(n)]
    for copy in reads:
        copy.start()
    for i in range(n):
        reads[i].wait()
        writes[i].start()
    for copy in writes:
        copy.wait()


def hand_on(*arrays):
    hbm = pl.BlockSpec(memory_space=pltpu.HBM)
    return pl.pallas_call(
        hand_on_kernel,
        out_shape=tuple(jax.ShapeDtypeStruct(a.shape, a.dtype) for a in arrays),
        in_specs=[hbm] * len(arrays),
        out_specs=(hbm,) * len(arrays),
        scratch_shapes=[VMEM(a.shape, a.dtype) for a in arrays] + [pltpu.SemaphoreType.DMA((2, len(arrays)))],
    )(*arrays)


def body(features, weight, bias, adj_blocks, block_rows, block_cols, block_counts, grad_out):
    nodes, hid = features.shape
    sem = pltpu.SemaphoreType.DMA
    block, thin = (EDGE, EDGE), (THIN, EDGE)
    vmem = pl.BlockSpec(memory_space=VMEM)
    hbm = pl.BlockSpec(memory_space=pltpu.HBM)
    hidden, grad_features, grad_weight, grad_bias = pl.pallas_call(
        layer_kernel,
        out_shape=(
            jax.ShapeDtypeStruct((nodes, hid), BF16),
            jax.ShapeDtypeStruct((nodes, hid), BF16),
            jax.ShapeDtypeStruct((hid, hid), F32),
            jax.ShapeDtypeStruct((1, hid), F32),
        ),
        in_specs=[vmem, vmem, vmem, hbm, hbm, vmem, hbm, hbm],
        out_specs=(hbm,) * 4,
        scratch_shapes=[
            VMEM((hid, hid), BF16),
            VMEM((nodes, hid), BF16),
            VMEM((nodes, hid), BF16),
            VMEM((nodes, hid), BF16),
            VMEM((hid, hid), F32),
            VMEM((1, hid), F32),
            SMEM((8, SLOTS), I32),
            SMEM((8, SLOTS), I32),
            VMEM((8, SLOTS), I32),
            VMEM((8, SLOTS), I32),
            VMEM((MAXB + 8, EDGE, EDGE), BF16),
            VMEM((COL_BLOCKS,) + block, BF16),
            VMEM((COL_BLOCKS,) + block, BF16),
            VMEM((FWD_STEPS,) + block, BF16),
            VMEM((BWD_STEPS,) + thin, BF16),
            VMEM((HALVES, 4, 4) + block, BF16),
            VMEM((HALVES, 4, 4) + block, BF16),
            VMEM((HALVES, 4, 4) + block, BF16),
            VMEM((HALVES, 4, 4) + block, BF16),
            VMEM((nodes, hid), F32),
            VMEM((nodes, hid), BF16),
            VMEM((ROW_BLOCKS,) + thin, BF16),
            VMEM((ROW_BLOCKS,) + thin, BF16),
            VMEM((ROW_BLOCKS,) + thin, BF16),
            VMEM((ROW_BLOCKS,) + thin, BF16),
            VMEM((CHUNKS, 2, 2, 4) + thin, BF16),
            VMEM((CHUNKS, 2, 2, 4) + thin, BF16),
            VMEM((CHUNKS, 2, 2, 2, 4) + thin, BF16),
            VMEM((CHUNKS, 2, 2, 2, 4) + thin, BF16),
            VMEM((CHUNKS, 2, 2, 4) + thin, BF16),
            VMEM((CHUNKS, 2, 4, 2) + thin, BF16),
            VMEM((CHUNKS, 2, 4, 2) + thin, BF16),
            VMEM((8, PART, hid), F32),
            VMEM((8, PART, hid), F32),
            VMEM((4, PART, hid), F32),
            VMEM((4, PART, hid), F32),
            VMEM((8, PART, hid), F32),
            sem, sem((HALVES,)), sem((2,)), sem((2,)), sem((4,)),
            sem((HALVES, 2, 19)), sem((HALVES, 2, 19)),
            sem((HALVES, 4)), sem((HALVES, 4)),
            sem((HALVES, 4)), sem((HALVES, 4)),
            sem((CHUNKS, 7)), sem((CHUNKS, 7)),
            sem((CHUNKS, 2, 6)), sem((CHUNKS, 2, 6)),
            sem((CHUNKS, 2, 4)), sem((CHUNKS, 2, 4)),
            sem((21,)), sem((21,)),
        ],
        compiler_params=pltpu.CompilerParams(
            collective_id=0, has_side_effects=True, vmem_limit_bytes=56 * 2**20
        ),
        cost_estimate=pl.CostEstimate(flops=8 * 10**9, bytes_accessed=16 * 2**20, transcendentals=2**18),
    )(
        block_counts, block_rows, block_cols, features.reshape(nodes // EDGE, EDGE, hid), weight,
        bias.reshape(1, hid), adj_blocks, grad_out,
    )
    hidden, grad_features, grad_weight, grad_bias = hand_on(hidden, grad_features, grad_weight, grad_bias)
    return hidden, grad_features, grad_weight, grad_bias.reshape(hid)


def solution(mesh):
    in_specs = (
        P(("row", "col"), None),
        P(),
        P(),
        P("row", "col", None, None, None),
        P("row", "col", None),
        P("row", "col", None),
        P("row", "col"),
        P(("row", "col"), None),
    )
    out_specs = (P(("row", "col"), None), P(("row", "col"), None), P(), P())
    return jax.shard_map(body, mesh=mesh, in_specs=in_specs, out_specs=out_specs, check_vma=False)
```

```python
import functools

import jax
import jax.numpy as jnp
from jax import lax
from jax.experimental import pallas as pl
from jax.experimental.pallas import tpu as pltpu
from jax.sharding import PartitionSpec as P

MESH = pl.DeviceIdType.MESH
VMEM = pltpu.VMEM
SMEM = pltpu.SMEM
BF16 = jnp.bfloat16
F32 = jnp.float32
I32 = jnp.int32
EDGE = 128
WIDE = 128
HALVES = 2
THIN = 64
CHUNKS = 4
SLOTS = 512
MAXB = 384
ROW_BLOCKS = 32
COL_BLOCKS = 64
FWD_STEPS = (MAXB + ROW_BLOCKS) // 2
BWD_STEPS = (MAXB + COL_BLOCKS) // 2
FWD_UNROLL = 26
BWD_UNROLL = 32
PART = 40


def dot(a, b):
    return jnp.dot(a, b, preferred_element_type=F32)


def dot_nt(a, b):
    return lax.dot_general(a, b, (((1,), (1,)), ((), ())), preferred_element_type=F32)


def dot_tn(a, b):
    return lax.dot_general(a, b, (((0,), (0,)), ((), ())), preferred_element_type=F32)


def one_table(outer, inner, count, table):
    ids = lax.broadcasted_iota(I32, (1, MAXB), 1)
    key = jnp.where(ids < count, outer, -1)
    turn = jnp.transpose(jnp.broadcast_to(key, (8, MAXB)))[:, 0:1]
    ones = jnp.ones((MAXB, MAXB), I32)
    earlier = lax.broadcasted_iota(I32, (MAXB, MAXB), 0) < lax.broadcasted_iota(I32, (MAXB, MAXB), 1)
    within = jnp.sum(jnp.where((turn == key) & earlier, ones, 0), axis=0, keepdims=True)
    lanes = lax.broadcasted_iota(I32, (MAXB, EDGE), 1)
    held = jnp.sum(jnp.where(turn == lanes, 1, 0), axis=0, keepdims=True)
    pairs = (held + 1) >> 1
    pairs_turn = jnp.transpose(jnp.broadcast_to(pairs, (8, EDGE)))[:, 0:1]
    rows = lax.broadcasted_iota(I32, (EDGE, EDGE), 0)
    upto = jnp.sum(jnp.where(rows <= lax.broadcasted_iota(I32, (EDGE, EDGE), 1), pairs_turn, 0), axis=0, keepdims=True)
    under = lax.broadcasted_iota(I32, (EDGE, MAXB), 0) < key
    start = jnp.sum(jnp.where(under, pairs_turn, 0), axis=0, keepdims=True)
    place = jnp.where(key >= 0, 2 * start + within, -1)
    packed = (ids + 1) + 512 * inner + jnp.where(within == 0, 65536, 0)
    place_turn = jnp.transpose(jnp.broadcast_to(place, (8, MAXB)))[:, 0:1]
    packed_turn = jnp.transpose(jnp.broadcast_to(packed, (8, MAXB)))[:, 0:1]
    taken = place_turn == lax.broadcasted_iota(I32, (MAXB, SLOTS), 1)
    picked = jnp.sum(jnp.where(taken, packed_turn, 0), axis=0, keepdims=True)
    block = picked & 511
    table[0:1, :] = jnp.where(block > 0, block - 1, MAXB)
    table[1:2, :] = (picked >> 9) & 63
    table[2:3, :] = 1 - (picked >> 16)
    table[3:4, :] = jnp.broadcast_to(jnp.concatenate([jnp.maximum(upto - 1, 0)] * 4, axis=1), (1, SLOTS))
    table[4:5, :] = jnp.concatenate([jnp.minimum(held, 1)] * 4, axis=1)
    table[5:8, :] = jnp.zeros((3, SLOTS), I32)


def layer_kernel(
    count, rows, cols, feat_hbm, weight_hbm, bias, blocks_hbm, gout_hbm,
    hidden_hbm, gfeat_hbm, gweight_hbm, gbias_hbm,
    weight, gout, hidden, gfeat, gweight, gbias,
    fwd, bwd, fwd_made, bwd_made,
    blocks, x0, x1, segs, segs2, sib_out, sib_in, z_out, z_in, ax, gp, gt0, gt1, gt2, gt3,
    f_out, f_in, c_out, c_in, own, r_out, r_in,
    ar_mine, ar_cols, ar_x, ar_y, ar_all,
    blocks_sem, feat_sem, table_sem, other_sem, out_sem, x_send, x_recv, sib_send, sib_recv, z_send, z_recv, g_send, g_recv,
    c_send, c_recv, r_send, r_recv, ar_send, ar_recv,
):
    row = lax.axis_index("row")
    col = lax.axis_index("col")
    x, y = row // 4, row % 4
    z, core = col // 2, col % 2
    xs = (x0, x1)
    gts = (gt0, gt1, gt2, gt3)

    def at_x(d):
        return (lax.rem(x + d + 4, 4) * 4 + y, col)

    def at_y(d):
        return (x * 4 + lax.rem(y + d + 4, 4), col)

    def at_z(d):
        return (row, lax.rem(z + d + 4, 4) * 2 + core)

    sibling = (row, z * 2 + 1 - core)

    def remote(src, dst, send, recv, to):
        return pltpu.make_async_remote_copy(
            src_ref=src, dst_ref=dst, send_sem=send, recv_sem=recv, device_id=to, device_id_type=MESH
        )

    load = pltpu.make_async_copy(blocks_hbm.at[0, 0], blocks.at[pl.ds(0, MAXB)], blocks_sem)
    base = (x * 4 + y) * 4
    feats = [
        pltpu.make_async_copy(
            feat_hbm.at[:, :, pl.ds(h * WIDE, WIDE)], xs[h].at[pl.ds(base, 4)], feat_sem.at[h]
        )
        for h in range(HALVES)
    ]
    for copy in feats:
        copy.start()
    others = [
        pltpu.make_async_copy(weight_hbm, weight, other_sem.at[0]),
        pltpu.make_async_copy(gout_hbm, gout, other_sem.at[1]),
    ]
    for copy in others:
        copy.start()
    load.start()
    results = [
        pltpu.make_async_copy(ref, hbm, out_sem.at[i])
        for i, (ref, hbm) in enumerate(
            ((hidden, hidden_hbm), (gfeat, gfeat_hbm), (gweight, gweight_hbm), (gbias, gbias_hbm))
        )
    ]
    barrier = pltpu.get_barrier_semaphore()
    for d in range(1, 4):
        for to in (at_x(d), at_y(d)):
            pl.semaphore_signal(barrier, inc=1, device_id=to, device_id_type=MESH)
    for d in range(1, 8):
        to = (row, lax.rem(col + d, 8))
        pl.semaphore_signal(barrier, inc=1, device_id=to, device_id_type=MESH)

    pl.semaphore_wait(barrier, 13)

    def slab(h, half, e, d):
        first = lax.rem((x if half == 0 else y) - e + 4, 4)
        second = lax.rem((y if half == 0 else x) - d + 4, 4)
        return (first, second) if half == 0 else (second, first)

    def x_copy(h, half, e, d, q, n, sem, to):
        i, j = slab(h, half, e, d)
        part = xs[h].at[pl.ds((i * 4 + j) * 4 + q, n)]
        return remote(part, part, x_send.at[h, half, sem], x_recv.at[h, half, sem], to)

    firsts = (at_x, at_y)
    seconds = (at_y, at_x)

    def x_along(h, half, d):
        return x_copy(h, half, 0, 0, 2 * half, 2, d - 1, firsts[half](d))

    def x_across(h, half, e, way):
        return x_copy(h, half, e, 0, 2 * half, 2, 3 + e * 4 + way, seconds[half](1 - 2 * way))

    def x_pass(h, half, e, way):
        return x_copy(
            h, half, e, 1 - 2 * way, 2 * half + way, 1, 5 + e * 4 + way, seconds[half](1 - 2 * way)
        )

    def x_relay(h, half, way):
        return x_copy(
            h, half, 1 - 2 * way, 0, 2 * half + way, 1, 1 + 18 * way, firsts[half](1 - 2 * way)
        )

    def x_start(h):
        for half in range(2):
            for d in (1, 3):
                x_along(h, half, d).start()
            for way in range(2):
                x_across(h, half, 0, way).start()

    def x_relay_start(h):
        for half in range(2):
            for way in range(2):
                x_along(h, half, 1 + 2 * way).wait_recv()
                x_relay(h, half, way).start()

    def x_step(h, e):
        for half in range(2):
            if e == 2:
                for way in range(2):
                    x_relay(h, half, way).wait_recv()
            for way in range(2):
                x_across(h, half, e, way).start()

    def x_forward(h, e):
        for half in range(2):
            for way in range(2):
                x_across(h, half, e, way).wait_recv()
                x_pass(h, half, e, way).start()

    def x_finish(h):
        for e in range(4):
            for half in range(2):
                for way in range(2):
                    x_pass(h, half, e, way).wait_recv()

    def x_drain(h):
        for half in range(2):
            for d in (1, 3):
                x_along(h, half, d).wait_send()
            for way in range(2):
                x_relay(h, half, way).wait_send()
            for e in range(4):
                for way in range(2):
                    x_across(h, half, e, way).wait_send()
                    x_pass(h, half, e, way).wait_send()

    def products(table, steps, unroll, wide, one, out, between):
        trips = steps // unroll
        cuts = [trips * i // len(between) for i in range(len(between) + 1)]

        def trip(i, acc):
            for u in range(unroll):
                k = i * unroll + u
                keep = table[2, 2 * k].astype(F32)
                acc = acc * keep + one(table[0, 2 * k], table[0, 2 * k + 1], table[1, 2 * k], table[1, 2 * k + 1])
                out[k] = acc.astype(BF16)
            return acc

        acc = jnp.zeros((wide, EDGE), F32)
        for i, act in enumerate(between):
            act()
            acc = lax.fori_loop(cuts[i], cuts[i + 1], trip, acc)

    def forward(h, between):
        def one(b0, b1, c0, c1):
            pair = jnp.concatenate([blocks[b0], blocks[b1]], axis=1)
            taken = jnp.concatenate([xs[h][c0], xs[h][c1]], axis=0)
            return dot(pair, taken)

        products(fwd, FWD_STEPS, FWD_UNROLL, EDGE, one, segs, between)

    def backward(h, between):
        def one(b0, b1, r0, r1):
            pair = jnp.concatenate([blocks[b0], blocks[b1]], axis=0)
            taken = jnp.concatenate([gts[h][r0], gts[h][r1]], axis=1)
            return dot(taken, pair)

        products(bwd, BWD_STEPS, BWD_UNROLL, THIN, one, segs2, between)

    def segment(table, out, r):
        return out[table[3, r]] * table[4, r].astype(F32).astype(BF16)

    def sib_copy(h, d):
        return remote(sib_out.at[h, d], sib_in.at[h, d], sib_send.at[h, d], sib_recv.at[h, d], sibling)

    def z_copy(h, d):
        return remote(z_out.at[h, d], z_in.at[h, d], z_send.at[h, d], z_recv.at[h, d], at_z(d))

    def sum_start(h):
        for d in (2, 1, 3, 0):
            zz = lax.rem(z + d, 4)
            for q in range(4):
                sib_out[h, d, q] = segment(fwd, segs, (zz * 2 + 1 - core) * 4 + q)
            sib_copy(h, d).start()
        for d in (1, 3, 2, 0):
            zz = lax.rem(z + d, 4)
            for q in range(4):
                z_out[h, d, q] = segment(fwd, segs, (zz * 2 + core) * 4 + q)

    def sum_step(h):
        for d in (2, 1, 3):
            sib_copy(h, d).wait_recv()
            for q in range(4):
                z_out[h, d, q] = (z_out[h, d, q].astype(F32) + sib_in[h, d, q].astype(F32)).astype(BF16)
            z_copy(h, d).start()
        sib_copy(h, 0).wait_recv()

    def sum_finish(h):
        for d in (1, 3, 2):
            z_copy(h, d).wait_recv()
        for q in range(4):
            total = z_out[h, 0, q].astype(F32) + sib_in[h, 0, q].astype(F32)
            for d in (1, 3, 2):
                total = total + z_in[h, d, q].astype(F32)
            ax[q * EDGE:(q + 1) * EDGE, h * WIDE:(h + 1) * WIDE] = total

    def g_part(h, d, k):
        return gts[h].at[pl.ds((lax.rem(z + d + 4, 4) * 2 + k) * 4, 4)]

    def g_across(h, d):
        part = g_part(h, 0, core)
        return remote(part, part, g_send.at[h, d - 1], g_recv.at[h, d - 1], at_z(d))

    def g_sibling(h, d):
        part = g_part(h, -d, core)
        return remote(part, part, g_send.at[h, 3 + d], g_recv.at[h, 3 + d], sibling)

    def g_start(h):
        for d in (2, 1, 3):
            g_across(h, d).start()
        g_sibling(h, 0).start()

    def g_step(h):
        for d in (1, 3, 2):
            g_across(h, d).wait_recv()
            g_sibling(h, d).start()
        for d in (0, 1, 3, 2):
            g_sibling(h, d).wait_recv()

    def f_copy(h, half, way):
        return remote(
            f_out.at[h, half, way], f_in.at[h, half, way],
            c_send.at[h, half, way], c_recv.at[h, half, way], firsts[half](1 - 2 * way),
        )

    def c_copy(h, half, way, q):
        return remote(
            c_out.at[h, half, way, q], c_in.at[h, half, way, q],
            c_send.at[h, half, 2 + 2 * way + q], c_recv.at[h, half, 2 + 2 * way + q], firsts[half](1 - 2 * way),
        )

    def r_copy(h, half, d):
        return remote(
            r_out.at[h, half, d], r_in.at[h, half, d], r_send.at[h, half, d], r_recv.at[h, half, d], seconds[half](d)
        )

    def back_gather(half, d, q, to):
        for s in range(4):
            first = lax.rem((x if half == 0 else y) + d + 4, 4)
            second = lax.rem((y if half == 0 else x) + s, 4)
            i, j = (first, second) if half == 0 else (second, first)
            to[s] = segment(bwd, segs2, (i * 4 + j) * 4 + 2 * half + q)

    def back_start(h):
        for half in range(2):
            for way in range(2):
                back_gather(half, 2, way, f_out.at[h, half, way])
                f_copy(h, half, way).start()
        for half in range(2):
            for way in range(2):
                back_gather(half, 1 - 2 * way, 1 - way, c_out.at[h, half, way, 1 - way])
                c_copy(h, half, way, 1 - way).start()
        for half in range(2):
            for way in range(2):
                back_gather(half, 1 - 2 * way, way, c_out.at[h, half, way, way])
        for half in range(2):
            for q in range(2):
                back_gather(half, 0, q, own.at[h, half, q])

    def back_pass(h):
        for half in range(2):
            for way in range(2):
                f_copy(h, half, way).wait_recv()
                for s in range(4):
                    c_out[h, half, way, way, s] = (
                        c_out[h, half, way, way, s].astype(F32) + f_in[h, half, way, s].astype(F32)
                    ).astype(BF16)
                c_copy(h, half, way, way).start()

    def back_step(h):
        for half in range(2):
            for way in range(2):
                for q in range(2):
                    c_copy(h, half, way, q).wait_recv()
            for s in (2, 1, 3, 0):
                for q in range(2):
                    total = own[h, half, q, s].astype(F32)
                    total = total + c_in[h, half, 0, q, s].astype(F32) + c_in[h, half, 1, q, s].astype(F32)
                    r_out[h, half, s, q] = total.astype(BF16)
                if s:
                    r_copy(h, half, s).start()

    def back_finish(h):
        for half in range(2):
            for d in (1, 3, 2):
                r_copy(h, half, d).wait_recv()
            for q in range(2):
                total = r_out[h, half, 0, q].astype(F32)
                for d in (1, 3, 2):
                    total = total + r_in[h, half, d, q].astype(F32)
                b = 2 * half + q
                gfeat[b * EDGE:(b + 1) * EDGE, h * THIN:(h + 1) * THIN] = jnp.transpose(total).astype(BF16)

    def ar_scatter(d):
        to = lax.rem(col + d, 8)
        return remote(ar_mine.at[to], ar_cols.at[col], ar_send.at[d], ar_recv.at[d], (row, to))

    def ar_over_x(d):
        return remote(ar_x.at[x], ar_x.at[x], ar_send.at[7 + d], ar_recv.at[7 + d], at_x(d))

    def ar_over_y(d):
        return remote(ar_y.at[y], ar_y.at[y], ar_send.at[10 + d], ar_recv.at[10 + d], at_y(d))

    def ar_gather(d):
        to = lax.rem(col + d, 8)
        return remote(ar_all.at[col], ar_all.at[col], ar_send.at[13 + d], ar_recv.at[13 + d], (row, to))

    def ar_start():
        for d in range(1, 8):
            ar_scatter(d).start()
        ar_cols[col] = ar_mine[col]

    def ar_step1():
        for d in range(1, 8):
            ar_scatter(d).wait_recv()
        total = ar_cols[0]
        for i in range(1, 8):
            total = total + ar_cols[i]
        ar_x[x] = total
        for d in range(1, 4):
            ar_over_x(d).start()

    def ar_step2():
        for d in range(1, 4):
            ar_over_x(d).wait_recv()
        ar_y[y] = (ar_x[0] + ar_x[1]) + (ar_x[2] + ar_x[3])
        for d in range(1, 4):
            ar_over_y(d).start()

    def ar_step3():
        for d in range(1, 4):
            ar_over_y(d).wait_recv()
        ar_all[col] = (ar_y[0] + ar_y[1]) + (ar_y[2] + ar_y[3])
        for d in range(1, 8):
            ar_gather(d).start()

    def ar_finish():
        for d in range(1, 8):
            ar_gather(d).wait_recv()
        for i in range(8):
            gweight[i * 32:(i + 1) * 32, :] = ar_all[i, 0:32, :]
        gbias[...] = ar_all[0, 32:33, :]

    def nothing():
        pass

    feats[0].wait()
    x_start(0)
    feats[1].wait()
    x_start(1)
    blocks[MAXB] = jnp.zeros((EDGE, EDGE), BF16)
    one_table(rows[0], cols[0], count[0:1, 0:1], fwd_made)
    put_fwd = pltpu.make_async_copy(fwd_made, fwd, table_sem.at[0])
    put_fwd.start()
    x_relay_start(0)
    for e in (1, 3):
        x_step(0, e)
    x_relay_start(1)
    x_step(0, 2)
    one_table(cols[0], rows[0], count[0:1, 0:1], bwd_made)
    put_bwd = pltpu.make_async_copy(bwd_made, bwd, table_sem.at[1])
    put_bwd.start()
    for e in (0, 1, 3, 2):
        x_forward(0, e)
    for e in (1, 3, 2):
        x_step(1, e)
    x_finish(0)
    put_fwd.wait()
    put_bwd.wait()
    load.wait()
    for copy in others:
        copy.wait()
    forward(0, [functools.partial(x_forward, 1, e) for e in (0, 1, 3, 2)] + [nothing])
    sum_start(0)
    sum_step(0)
    x_finish(1)
    forward(1, [nothing])
    sum_start(1)
    sum_step(1)
    sum_finish(0)
    sum_finish(1)

    bias_sum = jnp.zeros((1, HALVES * WIDE), F32)
    for q in range(4):
        at = slice(q * EDGE, (q + 1) * EDGE)
        total = ax[at, :]
        high = total.astype(BF16)
        low = (total - high.astype(F32)).astype(BF16)
        value = dot(high, weight[...]) + dot(low, weight[...]) + bias[...]
        sig = 1.0 / (1.0 + jnp.exp(-value))
        grad = (gout[at, :].astype(F32) * (sig * (1.0 + value * (1.0 - sig)))).astype(BF16)
        hidden[at, :] = (value * sig).astype(BF16)
        gp[at, :] = grad
        bias_sum = bias_sum + jnp.sum(grad.astype(F32), axis=0, keepdims=True)
        turned = dot_nt(weight[...], grad).astype(BF16)
        for h in range(CHUNKS):
            gts[h][col * 4 + q] = turned[h * THIN:(h + 1) * THIN, :]
    for h in range(CHUNKS):
        g_start(h)
    total = ax[...]
    high = total.astype(BF16)
    low = (total - high.astype(F32)).astype(BF16)
    weight_term = dot_tn(high, gp[...]) + dot_tn(low, gp[...])
    for i in range(8):
        ar_mine[i, 0:32, :] = weight_term[i * 32:(i + 1) * 32, :]
        ar_mine[i, 32:PART, :] = jnp.broadcast_to(bias_sum, (PART - 32, HALVES * WIDE))
    results[0].start()
    g_step(0)
    backward(0, [nothing])
    back_start(0)
    ar_start()
    g_step(1)
    backward(1, [nothing])
    back_pass(0)
    back_start(1)
    ar_step1()
    g_step(2)
    backward(2, [nothing])
    back_pass(1)
    back_step(0)
    back_start(2)
    ar_step2()
    g_step(3)
    backward(3, [nothing])
    back_pass(2)
    back_step(1)
    back_start(3)
    ar_step3()
    back_finish(0)
    back_pass(3)
    back_step(2)
    back_finish(1)
    ar_finish()
    results[2].start()
    results[3].start()
    back_step(3)
    back_finish(2)
    back_finish(3)
    results[1].start()

    for h in range(HALVES):
        x_drain(h)
        for d in range(4):
            sib_copy(h, d).wait_send()
        for d in range(1, 4):
            z_copy(h, d).wait_send()
    for h in range(CHUNKS):
        for d in range(4):
            g_sibling(h, d).wait_send()
        for d in range(1, 4):
            g_across(h, d).wait_send()
            for half in range(2):
                r_copy(h, half, d).wait_send()
        for half in range(2):
            for way in range(2):
                f_copy(h, half, way).wait_send()
                for q in range(2):
                    c_copy(h, half, way, q).wait_send()
    for d in range(1, 4):
        ar_over_x(d).wait_send()
        ar_over_y(d).wait_send()
    for d in range(1, 8):
        ar_scatter(d).wait_send()
        ar_gather(d).wait_send()
    for copy in results:
        copy.wait()


def hand_on_kernel(*refs):
    n = len(refs) // 3
    given, out, held, sems = refs[:n], refs[n:2 * n], refs[2 * n:3 * n], refs[3 * n]
    reads = [pltpu.make_async_copy(given[i], held[i], sems.at[0, i]) for i in range(n)]
    writes = [pltpu.make_async_copy(held[i], out[i], sems.at[1, i]) for i in range(n)]
    for copy in reads:
        copy.start()
    for i in range(n):
        reads[i].wait()
        writes[i].start()
    for copy in writes:
        copy.wait()


def hand_on(*arrays):
    hbm = pl.BlockSpec(memory_space=pltpu.HBM)
    return pl.pallas_call(
        hand_on_kernel,
        out_shape=tuple(jax.ShapeDtypeStruct(a.shape, a.dtype) for a in arrays),
        in_specs=[hbm] * len(arrays),
        out_specs=(hbm,) * len(arrays),
        scratch_shapes=[VMEM(a.shape, a.dtype) for a in arrays] + [pltpu.SemaphoreType.DMA((2, len(arrays)))],
    )(*arrays)


def body(features, weight, bias, adj_blocks, block_rows, block_cols, block_counts, grad_out):
    nodes, hid = features.shape
    sem = pltpu.SemaphoreType.DMA
    block, thin = (EDGE, EDGE), (THIN, EDGE)
    vmem = pl.BlockSpec(memory_space=VMEM)
    hbm = pl.BlockSpec(memory_space=pltpu.HBM)
    hidden, grad_features, grad_weight, grad_bias = pl.pallas_call(
        layer_kernel,
        out_shape=(
            jax.ShapeDtypeStruct((nodes, hid), BF16),
            jax.ShapeDtypeStruct((nodes, hid), BF16),
            jax.ShapeDtypeStruct((hid, hid), F32),
            jax.ShapeDtypeStruct((1, hid), F32),
        ),
        in_specs=[vmem, vmem, vmem, hbm, hbm, vmem, hbm, hbm],
        out_specs=(hbm,) * 4,
        scratch_shapes=[
            VMEM((hid, hid), BF16),
            VMEM((nodes, hid), BF16),
            VMEM((nodes, hid), BF16),
            VMEM((nodes, hid), BF16),
            VMEM((hid, hid), F32),
            VMEM((1, hid), F32),
            SMEM((8, SLOTS), I32),
            SMEM((8, SLOTS), I32),
            VMEM((8, SLOTS), I32),
            VMEM((8, SLOTS), I32),
            VMEM((MAXB + 8, EDGE, EDGE), BF16),
            VMEM((COL_BLOCKS,) + block, BF16),
            VMEM((COL_BLOCKS,) + block, BF16),
            VMEM((FWD_STEPS,) + block, BF16),
            VMEM((BWD_STEPS,) + thin, BF16),
            VMEM((HALVES, 4, 4) + block, BF16),
            VMEM((HALVES, 4, 4) + block, BF16),
            VMEM((HALVES, 4, 4) + block, BF16),
            VMEM((HALVES, 4, 4) + block, BF16),
            VMEM((nodes, hid), F32),
            VMEM((nodes, hid), BF16),
            VMEM((ROW_BLOCKS,) + thin, BF16),
            VMEM((ROW_BLOCKS,) + thin, BF16),
            VMEM((ROW_BLOCKS,) + thin, BF16),
            VMEM((ROW_BLOCKS,) + thin, BF16),
            VMEM((CHUNKS, 2, 2, 4) + thin, BF16),
            VMEM((CHUNKS, 2, 2, 4) + thin, BF16),
            VMEM((CHUNKS, 2, 2, 2, 4) + thin, BF16),
            VMEM((CHUNKS, 2, 2, 2, 4) + thin, BF16),
            VMEM((CHUNKS, 2, 2, 4) + thin, BF16),
            VMEM((CHUNKS, 2, 4, 2) + thin, BF16),
            VMEM((CHUNKS, 2, 4, 2) + thin, BF16),
            VMEM((8, PART, hid), F32),
            VMEM((8, PART, hid), F32),
            VMEM((4, PART, hid), F32),
            VMEM((4, PART, hid), F32),
            VMEM((8, PART, hid), F32),
            sem, sem((HALVES,)), sem((2,)), sem((2,)), sem((4,)),
            sem((HALVES, 2, 20)), sem((HALVES, 2, 20)),
            sem((HALVES, 4)), sem((HALVES, 4)),
            sem((HALVES, 4)), sem((HALVES, 4)),
            sem((CHUNKS, 7)), sem((CHUNKS, 7)),
            sem((CHUNKS, 2, 6)), sem((CHUNKS, 2, 6)),
            sem((CHUNKS, 2, 4)), sem((CHUNKS, 2, 4)),
            sem((21,)), sem((21,)),
        ],
        compiler_params=pltpu.CompilerParams(
            collective_id=0, has_side_effects=True, vmem_limit_bytes=56 * 2**20
        ),
        cost_estimate=pl.CostEstimate(flops=8 * 10**9, bytes_accessed=16 * 2**20, transcendentals=2**18),
    )(
        block_counts, block_rows, block_cols, features.reshape(nodes // EDGE, EDGE, hid), weight,
        bias.reshape(1, hid), adj_blocks, grad_out,
    )
    hidden, grad_features, grad_weight, grad_bias = hand_on(hidden, grad_features, grad_weight, grad_bias)
    return hidden, grad_features, grad_weight, grad_bias.reshape(hid)


def solution(mesh):
    in_specs = (
        P(("row", "col"), None),
        P(),
        P(),
        P("row", "col", None, None, None),
        P("row", "col", None),
        P("row", "col", None),
        P("row", "col"),
        P(("row", "col"), None),
    )
    out_specs = (P(("row", "col"), None), P(("row", "col"), None), P(), P())
    return jax.shard_map(body, mesh=mesh, in_specs=in_specs, out_specs=out_specs, check_vma=False)
```

```python
import functools

import jax
import jax.numpy as jnp
from jax import lax
from jax.experimental import pallas as pl
from jax.experimental.pallas import tpu as pltpu
from jax.sharding import PartitionSpec as P

MESH = pl.DeviceIdType.MESH
VMEM = pltpu.VMEM
SMEM = pltpu.SMEM
BF16 = jnp.bfloat16
F32 = jnp.float32
I32 = jnp.int32
EDGE = 128
WIDE = 128
HALVES = 2
THIN = 64
CHUNKS = 4
SLOTS = 512
MAXB = 384
ROW_BLOCKS = 32
COL_BLOCKS = 64
FWD_STEPS = (MAXB + ROW_BLOCKS) // 2
BWD_STEPS = (MAXB + COL_BLOCKS) // 2
FWD_UNROLL = 26
BWD_UNROLL = 32
PART = 40


def dot(a, b):
    return jnp.dot(a, b, preferred_element_type=F32)


def dot_nt(a, b):
    return lax.dot_general(a, b, (((1,), (1,)), ((), ())), preferred_element_type=F32)


def dot_tn(a, b):
    return lax.dot_general(a, b, (((0,), (0,)), ((), ())), preferred_element_type=F32)


def one_table(outer, inner, count, table):
    ids = lax.broadcasted_iota(I32, (1, MAXB), 1)
    key = jnp.where(ids < count, outer, -1)
    turn = jnp.transpose(jnp.broadcast_to(key, (8, MAXB)))[:, 0:1]
    ones = jnp.ones((MAXB, MAXB), I32)
    earlier = lax.broadcasted_iota(I32, (MAXB, MAXB), 0) < lax.broadcasted_iota(I32, (MAXB, MAXB), 1)
    within = jnp.sum(jnp.where((turn == key) & earlier, ones, 0), axis=0, keepdims=True)
    lanes = lax.broadcasted_iota(I32, (MAXB, EDGE), 1)
    held = jnp.sum(jnp.where(turn == lanes, 1, 0), axis=0, keepdims=True)
    pairs = (held + 1) >> 1
    pairs_turn = jnp.transpose(jnp.broadcast_to(pairs, (8, EDGE)))[:, 0:1]
    rows = lax.broadcasted_iota(I32, (EDGE, EDGE), 0)
    upto = jnp.sum(jnp.where(rows <= lax.broadcasted_iota(I32, (EDGE, EDGE), 1), pairs_turn, 0), axis=0, keepdims=True)
    under = lax.broadcasted_iota(I32, (EDGE, MAXB), 0) < key
    start = jnp.sum(jnp.where(under, pairs_turn, 0), axis=0, keepdims=True)
    place = jnp.where(key >= 0, 2 * start + within, -1)
    packed = (ids + 1) + 512 * inner + jnp.where(within == 0, 65536, 0)
    place_turn = jnp.transpose(jnp.broadcast_to(place, (8, MAXB)))[:, 0:1]
    packed_turn = jnp.transpose(jnp.broadcast_to(packed, (8, MAXB)))[:, 0:1]
    taken = place_turn == lax.broadcasted_iota(I32, (MAXB, SLOTS), 1)
    picked = jnp.sum(jnp.where(taken, packed_turn, 0), axis=0, keepdims=True)
    block = picked & 511
    table[0:1, :] = jnp.where(block > 0, block - 1, MAXB)
    table[1:2, :] = (picked >> 9) & 63
    table[2:3, :] = 1 - (picked >> 16)
    table[3:4, :] = jnp.broadcast_to(jnp.concatenate([jnp.maximum(upto - 1, 0)] * 4, axis=1), (1, SLOTS))
    table[4:5, :] = jnp.concatenate([jnp.minimum(held, 1)] * 4, axis=1)
    table[5:8, :] = jnp.zeros((3, SLOTS), I32)


def layer_kernel(
    count, rows, cols, feat_hbm, weight_hbm, bias, blocks_hbm, gout_hbm,
    hidden_hbm, gfeat_hbm, gweight_hbm, gbias_hbm,
    weight, gout, hidden, gfeat, gweight, gbias,
    fwd, bwd, fwd_made, bwd_made,
    blocks, x0, x1, segs, segs2, sib_out, sib_in, z_out, z_in, ax, gp, gt0, gt1, gt2, gt3,
    f_out, f_in, c_out, c_in, own, r_out, r_in,
    ar_mine, ar_cols, ar_x, ar_y, ar_all,
    blocks_sem, feat_sem, table_sem, other_sem, out_sem, x_send, x_recv, sib_send, sib_recv, z_send, z_recv, g_send, g_recv,
    c_send, c_recv, r_send, r_recv, ar_send, ar_recv,
):
    row = lax.axis_index("row")
    col = lax.axis_index("col")
    x, y = row // 4, row % 4
    z, core = col // 2, col % 2
    xs = (x0, x1)
    gts = (gt0, gt1, gt2, gt3)

    def at_x(d):
        return (lax.rem(x + d + 4, 4) * 4 + y, col)

    def at_y(d):
        return (x * 4 + lax.rem(y + d + 4, 4), col)

    def at_z(d):
        return (row, lax.rem(z + d + 4, 4) * 2 + core)

    sibling = (row, z * 2 + 1 - core)

    def remote(src, dst, send, recv, to):
        return pltpu.make_async_remote_copy(
            src_ref=src, dst_ref=dst, send_sem=send, recv_sem=recv, device_id=to, device_id_type=MESH
        )

    load = pltpu.make_async_copy(blocks_hbm.at[0, 0], blocks.at[pl.ds(0, MAXB)], blocks_sem)
    base = (x * 4 + y) * 4
    feats = [
        pltpu.make_async_copy(
            feat_hbm.at[:, :, pl.ds(h * WIDE, WIDE)], xs[h].at[pl.ds(base, 4)], feat_sem.at[h]
        )
        for h in range(HALVES)
    ]
    for copy in feats:
        copy.start()
    others = [
        pltpu.make_async_copy(weight_hbm, weight, other_sem.at[0]),
        pltpu.make_async_copy(gout_hbm, gout, other_sem.at[1]),
    ]
    for copy in others:
        copy.start()
    load.start()
    results = [
        pltpu.make_async_copy(ref, hbm, out_sem.at[i])
        for i, (ref, hbm) in enumerate(
            ((hidden, hidden_hbm), (gfeat, gfeat_hbm), (gweight, gweight_hbm), (gbias, gbias_hbm))
        )
    ]
    barrier = pltpu.get_barrier_semaphore()
    for d in range(1, 4):
        for to in (at_x(d), at_y(d)):
            pl.semaphore_signal(barrier, inc=1, device_id=to, device_id_type=MESH)
    for d in range(1, 8):
        to = (row, lax.rem(col + d, 8))
        pl.semaphore_signal(barrier, inc=1, device_id=to, device_id_type=MESH)

    pl.semaphore_wait(barrier, 13)

    def slab(h, half, e, d):
        first = lax.rem((x if half == 0 else y) - e + 4, 4)
        second = lax.rem((y if half == 0 else x) - d + 4, 4)
        return (first, second) if half == 0 else (second, first)

    def x_copy(h, half, e, d, q, n, sem, to):
        i, j = slab(h, half, e, d)
        part = xs[h].at[pl.ds((i * 4 + j) * 4 + q, n)]
        return remote(part, part, x_send.at[h, half, sem], x_recv.at[h, half, sem], to)

    firsts = (at_x, at_y)
    seconds = (at_y, at_x)

    def x_along(h, half, d):
        return x_copy(h, half, 0, 0, 2 * half, 2, d - 1, firsts[half](d))

    def x_across(h, half, e, way):
        return x_copy(h, half, e, 0, 2 * half, 2, 3 + e * 4 + way, seconds[half](1 - 2 * way))

    def x_pass(h, half, e, way):
        return x_copy(
            h, half, e, 1 - 2 * way, 2 * half + way, 1, 5 + e * 4 + way, seconds[half](1 - 2 * way)
        )

    def x_relay(h, half, way):
        return x_copy(
            h, half, 1 - 2 * way, 0, 2 * half + way, 1, 1 + 18 * way, firsts[half](1 - 2 * way)
        )

    def x_start(h):
        for half in range(2):
            for d in (1, 3):
                x_along(h, half, d).start()
            for way in range(2):
                x_across(h, half, 0, way).start()

    def x_relay_start(h):
        for half in range(2):
            for way in range(2):
                x_along(h, half, 1 + 2 * way).wait_recv()
                x_relay(h, half, way).start()

    def x_step(h, e):
        for half in range(2):
            if e == 2:
                for way in range(2):
                    x_relay(h, half, way).wait_recv()
            for way in range(2):
                x_across(h, half, e, way).start()

    def x_forward(h, e):
        for half in range(2):
            for way in range(2):
                x_across(h, half, e, way).wait_recv()
                x_pass(h, half, e, way).start()

    def x_finish(h):
        for e in range(4):
            for half in range(2):
                for way in range(2):
                    x_pass(h, half, e, way).wait_recv()

    def x_drain(h):
        for half in range(2):
            for d in (1, 3):
                x_along(h, half, d).wait_send()
            for way in range(2):
                x_relay(h, half, way).wait_send()
            for e in range(4):
                for way in range(2):
                    x_across(h, half, e, way).wait_send()
                    x_pass(h, half, e, way).wait_send()

    def products(table, steps, unroll, wide, one, out, between):
        trips = steps // unroll
        cuts = [trips * i // len(between) for i in range(len(between) + 1)]

        def trip(i, acc):
            for u in range(unroll):
                k = i * unroll + u
                keep = table[2, 2 * k].astype(F32)
                acc = acc * keep + one(table[0, 2 * k], table[0, 2 * k + 1], table[1, 2 * k], table[1, 2 * k + 1])
                out[k] = acc.astype(BF16)
            return acc

        acc = jnp.zeros((wide, EDGE), F32)
        for i, act in enumerate(between):
            act()
            acc = lax.fori_loop(cuts[i], cuts[i + 1], trip, acc)

    def forward(h, between):
        def one(b0, b1, c0, c1):
            pair = jnp.concatenate([blocks[b0], blocks[b1]], axis=1)
            taken = jnp.concatenate([xs[h][c0], xs[h][c1]], axis=0)
            return dot(pair, taken)

        products(fwd, FWD_STEPS, FWD_UNROLL, EDGE, one, segs, between)

    def backward(h, between):
        def one(b0, b1, r0, r1):
            pair = jnp.concatenate([blocks[b0], blocks[b1]], axis=0)
            taken = jnp.concatenate([gts[h][r0], gts[h][r1]], axis=1)
            return dot(taken, pair)

        products(bwd, BWD_STEPS, BWD_UNROLL, THIN, one, segs2, between)

    def segment(table, out, r):
        return out[table[3, r]] * table[4, r].astype(F32).astype(BF16)

    def sib_copy(h, d):
        return remote(sib_out.at[h, d], sib_in.at[h, d], sib_send.at[h, d], sib_recv.at[h, d], sibling)

    def z_copy(h, d):
        return remote(z_out.at[h, d], z_in.at[h, d], z_send.at[h, d], z_recv.at[h, d], at_z(d))

    def sum_start(h):
        for d in (2, 1, 3, 0):
            zz = lax.rem(z + d, 4)
            for q in range(4):
                sib_out[h, d, q] = segment(fwd, segs, (zz * 2 + 1 - core) * 4 + q)
            sib_copy(h, d).start()
        for d in (1, 3, 2, 0):
            zz = lax.rem(z + d, 4)
            for q in range(4):
                z_out[h, d, q] = segment(fwd, segs, (zz * 2 + core) * 4 + q)

    def sum_step(h):
        for d in (2, 1, 3):
            sib_copy(h, d).wait_recv()
            for q in range(4):
                z_out[h, d, q] = (z_out[h, d, q].astype(F32) + sib_in[h, d, q].astype(F32)).astype(BF16)
            z_copy(h, d).start()
        sib_copy(h, 0).wait_recv()

    def sum_finish(h):
        for d in (1, 3, 2):
            z_copy(h, d).wait_recv()
        for q in range(4):
            total = z_out[h, 0, q].astype(F32) + sib_in[h, 0, q].astype(F32)
            for d in (1, 3, 2):
                total = total + z_in[h, d, q].astype(F32)
            ax[q * EDGE:(q + 1) * EDGE, h * WIDE:(h + 1) * WIDE] = total

    def g_part(h, d, k):
        return gts[h].at[pl.ds((lax.rem(z + d + 4, 4) * 2 + k) * 4, 4)]

    def g_across(h, d):
        part = g_part(h, 0, core)
        return remote(part, part, g_send.at[h, d - 1], g_recv.at[h, d - 1], at_z(d))

    def g_sibling(h, d):
        part = g_part(h, -d, core)
        return remote(part, part, g_send.at[h, 3 + d], g_recv.at[h, 3 + d], sibling)

    def g_start(h):
        for d in (2, 1, 3):
            g_across(h, d).start()
        g_sibling(h, 0).start()

    def g_step(h):
        for d in (1, 3, 2):
            g_across(h, d).wait_recv()
            g_sibling(h, d).start()
        for d in (0, 1, 3, 2):
            g_sibling(h, d).wait_recv()

    def f_copy(h, half, way):
        return remote(
            f_out.at[h, half, way], f_in.at[h, half, way],
            c_send.at[h, half, way], c_recv.at[h, half, way], firsts[half](1 - 2 * way),
        )

    def c_copy(h, half, way, q):
        return remote(
            c_out.at[h, half, way, q], c_in.at[h, half, way, q],
            c_send.at[h, half, 2 + 2 * way + q], c_recv.at[h, half, 2 + 2 * way + q], firsts[half](1 - 2 * way),
        )

    def r_copy(h, half, d):
        return remote(
            r_out.at[h, half, d], r_in.at[h, half, d], r_send.at[h, half, d], r_recv.at[h, half, d], seconds[half](d)
        )

    def back_gather(half, d, q, to):
        for s in range(4):
            first = lax.rem((x if half == 0 else y) + d + 4, 4)
            second = lax.rem((y if half == 0 else x) + s, 4)
            i, j = (first, second) if half == 0 else (second, first)
            to[s] = segment(bwd, segs2, (i * 4 + j) * 4 + 2 * half + q)

    def back_start(h):
        for half in range(2):
            for way in range(2):
                back_gather(half, 2, way, f_out.at[h, half, way])
                f_copy(h, half, way).start()
        for half in range(2):
            for way in range(2):
                back_gather(half, 1 - 2 * way, 1 - way, c_out.at[h, half, way, 1 - way])
                c_copy(h, half, way, 1 - way).start()
        for half in range(2):
            for way in range(2):
                back_gather(half, 1 - 2 * way, way, c_out.at[h, half, way, way])
        for half in range(2):
            for q in range(2):
                back_gather(half, 0, q, own.at[h, half, q])

    def back_pass(h):
        for half in range(2):
            for way in range(2):
                f_copy(h, half, way).wait_recv()
                for s in range(4):
                    c_out[h, half, way, way, s] = (
                        c_out[h, half, way, way, s].astype(F32) + f_in[h, half, way, s].astype(F32)
                    ).astype(BF16)
                c_copy(h, half, way, way).start()

    def back_step(h):
        for half in range(2):
            for way in range(2):
                for q in range(2):
                    c_copy(h, half, way, q).wait_recv()
            for s in (2, 1, 3, 0):
                for q in range(2):
                    total = own[h, half, q, s].astype(F32)
                    total = total + c_in[h, half, 0, q, s].astype(F32) + c_in[h, half, 1, q, s].astype(F32)
                    r_out[h, half, s, q] = total.astype(BF16)
                if s:
                    r_copy(h, half, s).start()

    def back_finish(h):
        for half in range(2):
            for d in (1, 3, 2):
                r_copy(h, half, d).wait_recv()
            for q in range(2):
                total = r_out[h, half, 0, q].astype(F32)
                for d in (1, 3, 2):
                    total = total + r_in[h, half, d, q].astype(F32)
                b = 2 * half + q
                gfeat[b * EDGE:(b + 1) * EDGE, h * THIN:(h + 1) * THIN] = jnp.transpose(total).astype(BF16)

    def ar_scatter(d):
        to = lax.rem(col + d, 8)
        return remote(ar_mine.at[to], ar_cols.at[col], ar_send.at[d], ar_recv.at[d], (row, to))

    def ar_over_x(d):
        return remote(ar_x.at[x], ar_x.at[x], ar_send.at[7 + d], ar_recv.at[7 + d], at_x(d))

    def ar_over_y(d):
        return remote(ar_y.at[y], ar_y.at[y], ar_send.at[10 + d], ar_recv.at[10 + d], at_y(d))

    def ar_gather(d):
        to = lax.rem(col + d, 8)
        return remote(ar_all.at[col], ar_all.at[col], ar_send.at[13 + d], ar_recv.at[13 + d], (row, to))

    def ar_start():
        for d in range(1, 8):
            ar_scatter(d).start()
        ar_cols[col] = ar_mine[col]

    def ar_step1():
        for d in range(1, 8):
            ar_scatter(d).wait_recv()
        total = ar_cols[0]
        for i in range(1, 8):
            total = total + ar_cols[i]
        ar_x[x] = total
        for d in range(1, 4):
            ar_over_x(d).start()

    def ar_step2():
        for d in range(1, 4):
            ar_over_x(d).wait_recv()
        ar_y[y] = (ar_x[0] + ar_x[1]) + (ar_x[2] + ar_x[3])
        for d in range(1, 4):
            ar_over_y(d).start()

    def ar_step3():
        for d in range(1, 4):
            ar_over_y(d).wait_recv()
        ar_all[col] = (ar_y[0] + ar_y[1]) + (ar_y[2] + ar_y[3])
        for d in range(1, 8):
            ar_gather(d).start()

    def ar_finish():
        for d in range(1, 8):
            ar_gather(d).wait_recv()
        for i in range(8):
            gweight[i * 32:(i + 1) * 32, :] = ar_all[i, 0:32, :]
        gbias[...] = ar_all[0, 32:33, :]

    def nothing():
        pass

    feats[0].wait()
    x_start(0)
    feats[1].wait()
    x_start(1)
    blocks[MAXB] = jnp.zeros((EDGE, EDGE), BF16)
    one_table(rows[0], cols[0], count[0:1, 0:1], fwd_made)
    put_fwd = pltpu.make_async_copy(fwd_made, fwd, table_sem.at[0])
    put_fwd.start()
    x_relay_start(0)
    for e in (1, 3):
        x_step(0, e)
    x_relay_start(1)
    x_step(0, 2)
    one_table(cols[0], rows[0], count[0:1, 0:1], bwd_made)
    put_bwd = pltpu.make_async_copy(bwd_made, bwd, table_sem.at[1])
    put_bwd.start()
    for e in (0, 1, 3, 2):
        x_forward(0, e)
    for e in (1, 3, 2):
        x_step(1, e)
    x_finish(0)
    put_fwd.wait()
    put_bwd.wait()
    load.wait()
    for copy in others:
        copy.wait()
    forward(0, [functools.partial(x_forward, 1, e) for e in (0, 1, 3, 2)] + [nothing])
    sum_start(0)
    x_finish(1)
    forward(1, [functools.partial(sum_step, 0), nothing])
    sum_start(1)
    sum_step(1)
    sum_finish(0)
    sum_finish(1)

    bias_sum = jnp.zeros((1, HALVES * WIDE), F32)
    for q in range(4):
        at = slice(q * EDGE, (q + 1) * EDGE)
        total = ax[at, :]
        high = total.astype(BF16)
        low = (total - high.astype(F32)).astype(BF16)
        value = dot(high, weight[...]) + dot(low, weight[...]) + bias[...]
        sig = 1.0 / (1.0 + jnp.exp(-value))
        grad = (gout[at, :].astype(F32) * (sig * (1.0 + value * (1.0 - sig)))).astype(BF16)
        hidden[at, :] = (value * sig).astype(BF16)
        gp[at, :] = grad
        bias_sum = bias_sum + jnp.sum(grad.astype(F32), axis=0, keepdims=True)
        turned = dot_nt(weight[...], grad).astype(BF16)
        for h in range(CHUNKS):
            gts[h][col * 4 + q] = turned[h * THIN:(h + 1) * THIN, :]
    for h in range(CHUNKS):
        g_start(h)
    total = ax[...]
    high = total.astype(BF16)
    low = (total - high.astype(F32)).astype(BF16)
    weight_term = dot_tn(high, gp[...]) + dot_tn(low, gp[...])
    for i in range(8):
        ar_mine[i, 0:32, :] = weight_term[i * 32:(i + 1) * 32, :]
        ar_mine[i, 32:PART, :] = jnp.broadcast_to(bias_sum, (PART - 32, HALVES * WIDE))
    results[0].start()
    g_step(0)
    backward(0, [nothing])
    back_start(0)
    ar_start()
    g_step(1)
    backward(1, [nothing])
    back_pass(0)
    back_start(1)
    ar_step1()
    g_step(2)
    backward(2, [nothing])
    back_pass(1)
    back_step(0)
    back_start(2)
    ar_step2()
    g_step(3)
    backward(3, [nothing])
    back_pass(2)
    back_step(1)
    back_start(3)
    ar_step3()
    back_finish(0)
    back_pass(3)
    back_step(2)
    back_finish(1)
    ar_finish()
    results[2].start()
    results[3].start()
    back_step(3)
    back_finish(2)
    back_finish(3)
    results[1].start()

    for h in range(HALVES):
        x_drain(h)
        for d in range(4):
            sib_copy(h, d).wait_send()
        for d in range(1, 4):
            z_copy(h, d).wait_send()
    for h in range(CHUNKS):
        for d in range(4):
            g_sibling(h, d).wait_send()
        for d in range(1, 4):
            g_across(h, d).wait_send()
            for half in range(2):
                r_copy(h, half, d).wait_send()
        for half in range(2):
            for way in range(2):
                f_copy(h, half, way).wait_send()
                for q in range(2):
                    c_copy(h, half, way, q).wait_send()
    for d in range(1, 4):
        ar_over_x(d).wait_send()
        ar_over_y(d).wait_send()
    for d in range(1, 8):
        ar_scatter(d).wait_send()
        ar_gather(d).wait_send()
    for copy in results:
        copy.wait()


def hand_on_kernel(*refs):
    n = len(refs) // 3
    given, out, held, sems = refs[:n], refs[n:2 * n], refs[2 * n:3 * n], refs[3 * n]
    reads = [pltpu.make_async_copy(given[i], held[i], sems.at[0, i]) for i in range(n)]
    writes = [pltpu.make_async_copy(held[i], out[i], sems.at[1, i]) for i in range(n)]
    for copy in reads:
        copy.start()
    for i in range(n):
        reads[i].wait()
        writes[i].start()
    for copy in writes:
        copy.wait()


def hand_on(*arrays):
    hbm = pl.BlockSpec(memory_space=pltpu.HBM)
    return pl.pallas_call(
        hand_on_kernel,
        out_shape=tuple(jax.ShapeDtypeStruct(a.shape, a.dtype) for a in arrays),
        in_specs=[hbm] * len(arrays),
        out_specs=(hbm,) * len(arrays),
        scratch_shapes=[VMEM(a.shape, a.dtype) for a in arrays] + [pltpu.SemaphoreType.DMA((2, len(arrays)))],
    )(*arrays)


def body(features, weight, bias, adj_blocks, block_rows, block_cols, block_counts, grad_out):
    nodes, hid = features.shape
    sem = pltpu.SemaphoreType.DMA
    block, thin = (EDGE, EDGE), (THIN, EDGE)
    vmem = pl.BlockSpec(memory_space=VMEM)
    hbm = pl.BlockSpec(memory_space=pltpu.HBM)
    hidden, grad_features, grad_weight, grad_bias = pl.pallas_call(
        layer_kernel,
        out_shape=(
            jax.ShapeDtypeStruct((nodes, hid), BF16),
            jax.ShapeDtypeStruct((nodes, hid), BF16),
            jax.ShapeDtypeStruct((hid, hid), F32),
            jax.ShapeDtypeStruct((1, hid), F32),
        ),
        in_specs=[vmem, vmem, vmem, hbm, hbm, vmem, hbm, hbm],
        out_specs=(hbm,) * 4,
        scratch_shapes=[
            VMEM((hid, hid), BF16),
            VMEM((nodes, hid), BF16),
            VMEM((nodes, hid), BF16),
            VMEM((nodes, hid), BF16),
            VMEM((hid, hid), F32),
            VMEM((1, hid), F32),
            SMEM((8, SLOTS), I32),
            SMEM((8, SLOTS), I32),
            VMEM((8, SLOTS), I32),
            VMEM((8, SLOTS), I32),
            VMEM((MAXB + 8, EDGE, EDGE), BF16),
            VMEM((COL_BLOCKS,) + block, BF16),
            VMEM((COL_BLOCKS,) + block, BF16),
            VMEM((FWD_STEPS,) + block, BF16),
            VMEM((BWD_STEPS,) + thin, BF16),
            VMEM((HALVES, 4, 4) + block, BF16),
            VMEM((HALVES, 4, 4) + block, BF16),
            VMEM((HALVES, 4, 4) + block, BF16),
            VMEM((HALVES, 4, 4) + block, BF16),
            VMEM((nodes, hid), F32),
            VMEM((nodes, hid), BF16),
            VMEM((ROW_BLOCKS,) + thin, BF16),
            VMEM((ROW_BLOCKS,) + thin, BF16),
            VMEM((ROW_BLOCKS,) + thin, BF16),
            VMEM((ROW_BLOCKS,) + thin, BF16),
            VMEM((CHUNKS, 2, 2, 4) + thin, BF16),
            VMEM((CHUNKS, 2, 2, 4) + thin, BF16),
            VMEM((CHUNKS, 2, 2, 2, 4) + thin, BF16),
            VMEM((CHUNKS, 2, 2, 2, 4) + thin, BF16),
            VMEM((CHUNKS, 2, 2, 4) + thin, BF16),
            VMEM((CHUNKS, 2, 4, 2) + thin, BF16),
            VMEM((CHUNKS, 2, 4, 2) + thin, BF16),
            VMEM((8, PART, hid), F32),
            VMEM((8, PART, hid), F32),
            VMEM((4, PART, hid), F32),
            VMEM((4, PART, hid), F32),
            VMEM((8, PART, hid), F32),
            sem, sem((HALVES,)), sem((2,)), sem((2,)), sem((4,)),
            sem((HALVES, 2, 20)), sem((HALVES, 2, 20)),
            sem((HALVES, 4)), sem((HALVES, 4)),
            sem((HALVES, 4)), sem((HALVES, 4)),
            sem((CHUNKS, 7)), sem((CHUNKS, 7)),
            sem((CHUNKS, 2, 6)), sem((CHUNKS, 2, 6)),
            sem((CHUNKS, 2, 4)), sem((CHUNKS, 2, 4)),
            sem((21,)), sem((21,)),
        ],
        compiler_params=pltpu.CompilerParams(
            collective_id=0, has_side_effects=True, vmem_limit_bytes=56 * 2**20
        ),
        cost_estimate=pl.CostEstimate(flops=8 * 10**9, bytes_accessed=16 * 2**20, transcendentals=2**18),
    )(
        block_counts, block_rows, block_cols, features.reshape(nodes // EDGE, EDGE, hid), weight,
        bias.reshape(1, hid), adj_blocks, grad_out,
    )
    hidden, grad_features, grad_weight, grad_bias = hand_on(hidden, grad_features, grad_weight, grad_bias)
    return hidden, grad_features, grad_weight, grad_bias.reshape(hid)


def solution(mesh):
    in_specs = (
        P(("row", "col"), None),
        P(),
        P(),
        P("row", "col", None, None, None),
        P("row", "col", None),
        P("row", "col", None),
        P("row", "col"),
        P(("row", "col"), None),
    )
    out_specs = (P(("row", "col"), None), P(("row", "col"), None), P(), P())
    return jax.shard_map(body, mesh=mesh, in_specs=in_specs, out_specs=out_specs, check_vma=False)
```
